256 devices in a mesh: ens: 8 (over x, core), space: 32 (over y, z).
Axes of the slice: x: 4, y: 4, z: 8, core: 2. Of those that a mesh axis runs over, the one named last changes fastest.
Arguments:
- members_field: bfloat16 [512, 262144], P('ens', 'space'), may hold values from -6 to 6
- predicted: float32 [512, 40960], P('ens', 'space'), may hold values from -6 to 6
- noise: float32 [512, 40960], P('ens', 'space'), may hold values from -6 to 6
- observed: float32 [40960], P('space'), may hold values from -8 to 8
- obs_precision: float32 [40960], P('space'), may hold values from 0.5 to 2
- obs_block: int32 [40960], P('space'), may hold values from 0 to 31
- block_error_scale: float32 [32], replicated, may hold values from 0.5 to 2
- member_ids: int32 [512], replicated, may hold values from 0 to 511, each once
Outputs:
- updated_field: bfloat16 [512, 262144], P('ens', 'space')
The draws below stay inside these ranges and needn't reach their ends.
Inputs may be any that keep to these rules, and one draw needn't show every extreme that they name: `member_ids`: each member appears exactly once.
All inputs are finite; a program needn't handle non-finite values.
Results may differ from the reference program's by a relative error of at most 0.012.
The reference program's roundings to bfloat16 on the way (of `transform` and `anomaly`) count: a program that leaves them out, or rounds other values in their place, can miss the bound.
Values may be sent and summed in bfloat16 or wider, within the bound.
No kernel may reach another device: no remote copies, remote signals or barrier semaphores. Data moves between devices by JAX's collectives and lax.ppermute only.
A program may use at most 64 MiB of HBM per device.

```python
import math
import jax
import jax.numpy as jnp
from jax import lax

MEMBERS = 512
CC = 8192
BLOCKS = 32
CELLS = 262144
OBS = 40960
N_SPACE = 32


def place_ends(array, key, least, largest):
    longest = array.shape.index(max(array.shape))
    spots = []
    for shift in (0, 1):
        where = [jax.random.randint(jax.random.fold_in(key, axis), (), 0, length) for axis, length in enumerate(array.shape)]
        where[longest] = (where[longest] + shift) % array.shape[longest]
        spots.append(tuple(where))
    return array.at[spots[0]].set(least).at[spots[1]].set(largest)


def block_levels(rng, shape, split, least, top_value):
    def one(axis_at, shards_of):
        heights = jax.random.uniform(jax.random.fold_in(jax.random.fold_in(rng, 6), axis_at), (shards_of,), jnp.float32, least / len(split), top_value / len(split))
        return jnp.repeat(jnp.exp(heights), shape[axis_at] // shards_of).reshape((-1,) + (1,) * (len(shape) - axis_at - 1))

    factor_of = one(*split[0])
    for cut in split[1:]:
        factor_of = factor_of * one(*cut)
    return factor_of


def centred(key, dims, deviation, reach, pieces=(), kind=jnp.bfloat16):
    entries = deviation * jax.random.normal(key, dims, jnp.float32)
    if pieces:
        entries = entries * block_levels(key, dims, pieces, -0.22, 0.18)
    return jnp.clip(entries, -reach, reach).astype(kind)


def setup_inputs(seed: int = 0) -> dict:
    keys = jax.random.split(jax.random.key(seed), 9)
    return {
        "members_field": centred(keys[0], (MEMBERS, CELLS), 1.0, 6.0, ((0, 8), (1, 32))),
        "predicted": centred(keys[1], (MEMBERS, OBS), 1.0, 6.0, ((0, 8), (1, 32)), jnp.float32),
        "noise": centred(keys[2], (MEMBERS, OBS), 1.0, 6.0, ((0, 8), (1, 32)), jnp.float32),
        "observed": centred(keys[3], (OBS,), 1.5, 8.0, ((0, 32),), jnp.float32),
        "obs_precision": jnp.clip(jnp.exp(math.log(2.0) - 1.3862944 * jax.random.uniform(keys[4], (OBS,), jnp.float32) ** block_levels(keys[4], (OBS,), ((0, 32),), -0.2, 0.2)), 0.5, 2.0),
        "obs_block": place_ends(jax.random.randint(keys[5], (OBS,), 0, BLOCKS), jax.random.fold_in(keys[5], 1), 0, BLOCKS - 1).astype(jnp.int32),
        "block_error_scale": jnp.clip(jnp.exp(jax.random.uniform(keys[6], (BLOCKS,), jnp.float32, math.log(0.5), math.log(2.0))), 0.5, 2.0),
        "member_ids": jax.random.permutation(keys[7], MEMBERS).astype(jnp.int32),
    }


def reference(members_field, predicted, noise, observed, obs_precision, obs_block, block_error_scale, member_ids):
    hits = obs_block[:, None] == jnp.arange(BLOCKS, dtype=jnp.int32)[None, :]
    scale = lax.optimization_barrier(jnp.sum(jnp.where(hits, block_error_scale[None, :], jnp.zeros_like(block_error_scale)[None, :]), axis=1))
    weight = obs_precision / scale
    ordered = jnp.zeros_like(predicted).at[member_ids].set(predicted)
    factor = 1.0 / jnp.sqrt(jnp.float32(MEMBERS - 1))
    pred_mean = lax.optimization_barrier(jnp.mean(ordered, axis=0))
    spread = weight[None, :] * (ordered - pred_mean[None, :]) * factor
    innovation = (weight[None, :] * (observed[None, :] - ordered) + noise) * factor
    gram = jnp.dot(spread, spread.T, precision=lax.Precision.HIGHEST)
    cross = jnp.dot(spread, innovation.T, precision=lax.Precision.HIGHEST)
    system = jnp.eye(MEMBERS, dtype=gram.dtype) + gram
    lower = jnp.linalg.cholesky(system)
    transform = jax.scipy.linalg.cho_solve((lower, True), cross).astype(jnp.bfloat16)
    transposed = transform.T

    def one_block(index):
        block = lax.dynamic_slice_in_dim(members_field, index * CC, CC, 1)
        field_mean = lax.optimization_barrier(jnp.sum(block, axis=0, dtype=jnp.float32)) / MEMBERS
        anomaly = (block.astype(jnp.float32) - field_mean[None, :]).astype(jnp.bfloat16)
        increment = jnp.dot(transposed.astype(jnp.float32), anomaly.astype(jnp.float32), preferred_element_type=jnp.float32)
        return (block.astype(jnp.float32) + increment).astype(jnp.bfloat16)
    stacked = lax.map(one_block, jnp.arange(N_SPACE, dtype=jnp.int32))
    return jnp.transpose(stacked, (1, 0, 2)).reshape(MEMBERS, CELLS)
```

```python
import functools
import jax
import jax.numpy as jnp
from jax import lax
from jax.experimental import pallas as pl
from jax.experimental.pallas import tpu as pltpu
from jax.sharding import PartitionSpec as P

F32 = jnp.float32
BF16 = jnp.bfloat16
EXACT = lax.Precision.HIGHEST
MIB = 1024 * 1024


def across_rows(tile, row):
    return jnp.broadcast_to(tile[row : row + 1, :], tile.shape)


def across_lanes(tile, lane):
    return jnp.broadcast_to(tile[:, lane : lane + 1], tile.shape)


def dot_nt(a, b, precision=None):
    return lax.dot_general(
        a, b, (((1,), (1,)), ((), ())), precision=precision, preferred_element_type=F32
    )


def dot_nn(a, b, precision=None):
    return jnp.dot(a, b, precision=precision, preferred_element_type=F32)


def invert_block(block):
    lanes = lax.broadcasted_iota(jnp.int32, (8, 128), 1)
    subs = lax.broadcasted_iota(jnp.int32, (8, 128), 0)
    tiles = [block[8 * i : 8 * i + 8, :] for i in range(16)]
    for t in range(16):
        cols = [across_lanes(tiles[t], 8 * t + j) for j in range(8)]
        for k in range(8):
            recip = 1.0 / across_rows(cols[k], k)
            pivot = cols[k]
            here = subs == k
            for j in range(8):
                if j != k:
                    scaled = across_rows(cols[j], k) * recip
                    cols[j] = jnp.where(here, scaled, cols[j] - pivot * scaled)
            cols[k] = jnp.where(here, recip, -pivot * recip)
        panel = (lanes >= 8 * t) & (lanes < 8 * t + 8)
        old = tiles[t]
        row = cols[0] * across_rows(old, 0)
        for j in range(1, 8):
            row = row + cols[j] * across_rows(old, j)
        for j in range(8):
            row = jnp.where(lanes == 8 * t + j, cols[j], row)
        rows = [across_rows(row, j) for j in range(8)]
        for i in range(16):
            if i == t:
                continue
            terms = [across_lanes(tiles[i], 8 * t + j) * rows[j] for j in range(8)]
            pairs = [terms[j] + terms[j + 1] for j in range(0, 8, 2)]
            total = (pairs[0] + pairs[1]) + (pairs[2] + pairs[3])
            tiles[i] = jnp.where(panel, 0.0, tiles[i]) - total
        tiles[t] = row
    return jnp.concatenate(tiles, axis=0)


def prepare_kernel(mine_ref, got_ref, scale_ref, out_ref):
    mine = mine_ref[...]
    got = got_ref[...]
    rows = 2 * mine.shape[0]
    mean = (jnp.sum(mine, axis=0, keepdims=True) + jnp.sum(got, axis=0, keepdims=True)) / rows
    scale = scale_ref[...]
    half = mine.shape[0]
    out_ref[0:half, :] = ((mine - mean) * scale).astype(BF16)
    out_ref[half:rows, :] = ((got - mean) * scale).astype(BF16)
    high = mean.astype(BF16)
    rest = mean - high.astype(F32)
    mid = rest.astype(BF16)
    low = (rest - mid.astype(F32)).astype(BF16)
    out_ref[rows : rows + 16, :] = jnp.concatenate(
        [high, mid, low, jnp.zeros((13, mean.shape[1]), BF16)], axis=0
    )


def gram_kernel(p0_ref, p1_ref, p2_ref, p3_ref, mine_ref, got_ref, scale_ref, obs_ref, own_ref, other_ref, *, factor):
    refs = (p0_ref, p1_ref, p2_ref, p3_ref)
    rows = p0_ref.shape[0] - 16
    half = rows // 2
    scale = scale_ref[...]
    means = []
    for ref in refs:
        tail = ref[rows : rows + 16, :].astype(F32)
        means.append(tail[0:1, :] + (tail[1:2, :] + tail[2:3, :]))
    mean = ((means[0] + means[1]) + (means[2] + means[3])) * 0.25
    spreads = [
        (ref[0:rows, :].astype(F32) + scale * (m - mean)).astype(BF16) for ref, m in zip(refs, means)
    ]
    shift = scale * (obs_ref[...] - mean)
    noise = jnp.concatenate([mine_ref[...], got_ref[...]], axis=0)
    right = shift + factor * noise
    high = right.astype(BF16)
    low = (right - high.astype(F32)).astype(BF16)
    left = jnp.concatenate([spreads[0], high, low], axis=0)
    for i in range(4):
        part = dot_nt(left, spreads[i])
        gram = part[0:rows]
        cross = part[rows : 2 * rows] + part[2 * rows : 3 * rows]
        own_ref[i, 0:half, :] = gram[0:half]
        own_ref[i, half:rows, :] = cross[0:half]
        other_ref[i, 0:half, :] = pltpu.roll(gram[half:rows], half, 1)
        other_ref[i, half:rows, :] = pltpu.roll(cross[half:rows], half, 1)


def solve_kernel(
    first_ref, g0_ref, g1_ref, g2_ref, g3_ref, other_ref, cross_ref, ids_row_ref, ids_col_ref, out_ref, a_ref, m_ref
):
    size = 512
    block = 128
    half = 64
    first = first_ref[0]
    unit = (
        lax.broadcasted_iota(jnp.int32, (block, block), 0) == lax.broadcasted_iota(jnp.int32, (block, block), 1)
    ).astype(F32)
    own = (g0_ref, g1_ref, g2_ref, g3_ref)
    for k in range(4):
        for i in range(4):
            j = (i - k) % 4
            piece = jnp.concatenate([own[k][j], pltpu.roll(other_ref[k, j], half, 1)], axis=0)
            if i == k:
                piece = piece + unit
            a_ref[k * block : (k + 1) * block, i * block : (i + 1) * block] = piece
    members = first + lax.broadcasted_iota(jnp.int32, (half, block), 0)
    for i in range(4):
        ids = ids_row_ref[:, i * block : (i + 1) * block]
        m_ref[:, i * block : (i + 1) * block] = cross_ref[i] + (ids == members).astype(F32)

    inverses, uppers = [], []
    for b in range(4):
        lo, hi = b * block, (b + 1) * block
        inverse = invert_block(a_ref[lo:hi, lo:hi])
        inverses.append(inverse)
        if hi < size:
            upper = dot_nn(inverse, a_ref[lo:hi, hi:size], EXACT)
            uppers.append(upper)
            a_ref[hi:size, hi:size] = a_ref[hi:size, hi:size] - dot_nn(a_ref[hi:size, lo:hi], upper, EXACT)
            m_ref[:, hi:size] = m_ref[:, hi:size] - dot_nn(m_ref[:, lo:hi], upper, EXACT)
    for b in range(3, -1, -1):
        lo, hi = b * block, (b + 1) * block
        z = dot_nn(m_ref[:, lo:hi], inverses[b], EXACT)
        if hi < size:
            z = z - dot_nt(m_ref[:, hi:size], uppers[b], EXACT)
        m_ref[:, lo:hi] = z

    place = (ids_col_ref[...] == lax.broadcasted_iota(jnp.int32, (size, size), 1)).astype(F32)
    ordered = dot_nn(m_ref[...], place, EXACT)
    own_unit = (
        lax.broadcasted_iota(jnp.int32, (half, size), 1) == first + lax.broadcasted_iota(jnp.int32, (half, size), 0)
    ).astype(F32)
    out_ref[...] = (ordered - own_unit).astype(BF16)


def body(members_field, predicted, noise, observed, obs_precision, obs_block, block_error_scale, member_ids):
    rows, width = predicted.shape
    members = member_ids.shape[0]
    half = width // 2
    place = lax.axis_index("ens")
    core = lax.rem(place, 2)
    chip = lax.div(place, 2)
    swap = [(i, i ^ 1) for i in range(8)]

    def turned(array, steps):
        return lax.ppermute(array, "ens", [(i, (i + 2 * steps) % 8) for i in range(8)])

    def cut(array, which):
        return lax.dynamic_slice_in_dim(array, which * half, half, array.ndim - 1)

    field = lax.all_gather(members_field, "ens", axis=0, tiled=True)

    pred_mine, noise_mine = cut(predicted, core), cut(noise, core)
    pred_got = lax.ppermute(cut(predicted, 1 - core), "ens", swap)
    noise_got = lax.ppermute(cut(noise, 1 - core), "ens", swap)

    blocks = block_error_scale.shape[0]
    block_here = cut(obs_block, core)
    hits = block_here[None, :] == jnp.arange(blocks, dtype=jnp.int32)[:, None]
    error_scale = jnp.sum(jnp.where(hits, block_error_scale[:, None], 0.0), axis=0)
    factor = float(1.0 / (members - 1) ** 0.5)
    scale = (cut(obs_precision, core) / error_scale * factor)[None, :]
    obs_here = cut(observed, core)[None, :]

    payload = pl.pallas_call(
        prepare_kernel, out_shape=jax.ShapeDtypeStruct((2 * rows + 16, half), BF16), name="prepare"
    )(pred_mine, pred_got, scale)
    payloads = [payload] + [turned(payload, k) for k in (1, 2, 3)]
    shape = jax.ShapeDtypeStruct((4, 2 * rows, 2 * rows), F32)
    own, other = pl.pallas_call(
        functools.partial(gram_kernel, factor=factor), out_shape=(shape, shape), name="gram"
    )(*payloads, noise_mine, noise_got, scale, obs_here)
    part = own + lax.ppermute(other, "ens", swap)

    spread_out = lax.all_to_all(part.reshape(32, 16, 128), "space", split_axis=0, concat_axis=0)
    summed = jnp.sum(spread_out, axis=0)
    whole = lax.all_to_all(
        jnp.broadcast_to(summed[None], (32, 16, 128)), "space", split_axis=0, concat_axis=0
    ).reshape(4, 2 * rows, 2 * rows)
    gram = whole[:, :rows]
    cross = whole[:, rows:]
    grams = [gram] + [turned(gram, k) for k in (1, 2, 3)]
    others = lax.ppermute(jnp.stack(grams), "ens", swap)

    ids = member_ids.reshape(4, 2, rows)
    ids = jnp.stack(
        [
            lax.dynamic_slice(ids, (lax.rem(chip + 4 - k, 4), lax.rem(core + c, 2), 0), (1, 1, rows))[0, 0]
            for k in range(4)
            for c in range(2)
        ]
    ).reshape(members)
    first = (place * rows).reshape(1).astype(jnp.int32)
    vmem = pl.BlockSpec(memory_space=pltpu.VMEM)
    transform = pl.pallas_call(
        solve_kernel,
        out_shape=jax.ShapeDtypeStruct((rows, members), BF16),
        in_specs=[pl.BlockSpec(memory_space=pltpu.SMEM)] + [vmem] * 8,
        out_specs=vmem,
        scratch_shapes=[pltpu.VMEM((members, members), F32), pltpu.VMEM((rows, members), F32)],
        compiler_params=pltpu.CompilerParams(vmem_limit_bytes=32 * MIB),
        name="solve",
    )(first, *grams, others, cross, ids[None, :], ids[:, None])

    field_mean = jnp.sum(field, axis=0, dtype=F32) / members
    anomaly = (field.astype(F32) - field_mean[None, :]).astype(BF16)
    increment = jnp.dot(transform, anomaly, preferred_element_type=F32)
    return (members_field.astype(F32) + increment).astype(BF16)


def solution(mesh):
    placed = (
        P("ens", "space"),
        P("ens", "space"),
        P("ens", "space"),
        P("space"),
        P("space"),
        P("space"),
        P(),
        P(),
    )
    return jax.shard_map(
        body, mesh=mesh, in_specs=placed, out_specs=P("ens", "space"), check_vma=False
    )
```

```python
import functools
import jax
import jax.numpy as jnp
from jax import lax
from jax.experimental import pallas as pl
from jax.experimental.pallas import tpu as pltpu
from jax.sharding import PartitionSpec as P

F32 = jnp.float32
BF16 = jnp.bfloat16
EXACT = lax.Precision.HIGHEST
MIB = 1024 * 1024


def across_rows(tile, row):
    return jnp.broadcast_to(tile[row : row + 1, :], tile.shape)


def across_lanes(tile, lane):
    return jnp.broadcast_to(tile[:, lane : lane + 1], tile.shape)


def dot_nt(a, b, precision=None):
    return lax.dot_general(
        a, b, (((1,), (1,)), ((), ())), precision=precision, preferred_element_type=F32
    )


def dot_tn(a, b, precision=None):
    return lax.dot_general(
        a, b, (((0,), (0,)), ((), ())), precision=precision, preferred_element_type=F32
    )


def dot_nn(a, b, precision=None):
    return jnp.dot(a, b, precision=precision, preferred_element_type=F32)


def tree_sum(terms):
    while len(terms) > 1:
        terms = [terms[i] + terms[i + 1] if i + 1 < len(terms) else terms[i] for i in range(0, len(terms), 2)]
    return terms[0]


def unit_block(rows, cols):
    at = lax.broadcasted_iota(jnp.int32, (rows, cols), 0)
    return (at == lax.broadcasted_iota(jnp.int32, (rows, cols), 1)).astype(F32)


def invert_block(block):
    lanes = lax.broadcasted_iota(jnp.int32, (8, 128), 1)
    subs = lax.broadcasted_iota(jnp.int32, (8, 128), 0)
    tiles = [block[8 * i : 8 * i + 8, :] for i in range(16)]
    for t in range(16):
        old = tiles[t]
        cols = [across_lanes(old, 8 * t + j) for j in range(8)]
        panel = (lanes >= 8 * t) & (lanes < 8 * t + 8)
        old = jnp.where(panel, (lanes - 8 * t == subs).astype(F32), old)
        olds = [across_rows(old, j) for j in range(8)]
        for k in range(8):
            recip = 1.0 / across_rows(cols[k], k)
            pivot = cols[k]
            here = subs == k
            for j in range(8):
                if j != k:
                    scaled = across_rows(cols[j], k) * recip
                    cols[j] = jnp.where(here, scaled, cols[j] - pivot * scaled)
            cols[k] = jnp.where(here, recip, -pivot * recip)
        row = tree_sum([cols[j] * olds[j] for j in range(8)])
        rows = [across_rows(row, j) for j in range(8)]
        for i in [(t + 1 + n) % 16 for n in range(15)]:
            total = tree_sum([across_lanes(tiles[i], 8 * t + j) * rows[j] for j in range(8)])
            tiles[i] = jnp.where(panel, 0.0, tiles[i]) - total
        tiles[t] = row
    return jnp.concatenate(tiles, axis=0)


def prepare_kernel(place_ref, table_ref, mine_ref, got_ref, facts_ref, out_ref, side_ref, *, factor):
    half = mine_ref.shape[0]
    rows = 2 * half
    width = out_ref.shape[1]
    here = pl.ds(pl.multiple_of(lax.rem(place_ref[0], 2) * width, 128), width)
    block = facts_ref[2:3, here]
    error_scale = jnp.zeros_like(block)
    for b in range(table_ref.shape[0]):
        error_scale = jnp.where(block == float(b), table_ref[b], error_scale)
    scale = facts_ref[0:1, here] / error_scale * factor
    side_ref[...] = jnp.concatenate([scale, facts_ref[1:2, here], jnp.zeros((6, width), F32)], axis=0)
    mine = mine_ref[:, here]
    got = got_ref[:, here]
    mean = (jnp.sum(mine, axis=0, keepdims=True) + jnp.sum(got, axis=0, keepdims=True)) / rows
    out_ref[0:half, :] = ((mine - mean) * scale).astype(BF16)
    out_ref[half:rows, :] = ((got - mean) * scale).astype(BF16)
    high = mean.astype(BF16)
    rest = mean - high.astype(F32)
    mid = rest.astype(BF16)
    low = (rest - mid.astype(F32)).astype(BF16)
    out_ref[rows : rows + 16, :] = jnp.concatenate([high, mid, low, jnp.zeros((13, width), BF16)], axis=0)


def gram_kernel(
    place_ref, p0_ref, p1_ref, p2_ref, p3_ref, mine_ref, got_ref, side_ref, own_ref, other_ref, *, factor
):
    refs = (p0_ref, p1_ref, p2_ref, p3_ref)
    rows = p0_ref.shape[0] - 16
    half = rows // 2
    width = p0_ref.shape[1]
    here = pl.ds(pl.multiple_of(lax.rem(place_ref[0], 2) * width, 128), width)
    scale = side_ref[0:1, :]
    means = []
    for ref in refs:
        tail = ref[rows : rows + 16, :].astype(F32)
        means.append(tail[0:1, :] + (tail[1:2, :] + tail[2:3, :]))
    mean = ((means[0] + means[1]) + (means[2] + means[3])) * 0.25
    spreads = [
        (ref[0:rows, :].astype(F32) + scale * (m - mean)).astype(BF16) for ref, m in zip(refs, means)
    ]
    left_over = tree_sum([jnp.sum(s.astype(F32), axis=0, keepdims=True) for s in spreads]) / (4 * rows)
    over_high = left_over.astype(BF16)
    over_low = (left_over - over_high.astype(F32)).astype(BF16)
    over = jnp.concatenate([over_high, over_low, jnp.zeros((14, width), BF16)], axis=0)
    shift = scale * (side_ref[1:2, :] - mean)
    noise = jnp.concatenate([mine_ref[:, here], got_ref[:, here]], axis=0)
    right = shift + factor * noise
    high = right.astype(BF16)
    low = (right - high.astype(F32)).astype(BF16)
    left = jnp.concatenate([spreads[0], high, low, over], axis=0)
    at_over = dot_nt(left, over)
    at_over = at_over[:, 0:1] + at_over[:, 1:2]
    gram_over = at_over[0:rows]
    cross_over = at_over[rows : 2 * rows] + at_over[2 * rows : 3 * rows]
    both = at_over[3 * rows : 3 * rows + 1] + at_over[3 * rows + 1 : 3 * rows + 2]
    for i in range(4):
        part = dot_nt(left, spreads[i])
        over_row = part[3 * rows : 3 * rows + 1] + part[3 * rows + 1 : 3 * rows + 2]
        gram = part[0:rows] - gram_over - (over_row - both)
        cross = part[rows : 2 * rows] + part[2 * rows : 3 * rows] - cross_over
        own_ref[i, 0:half, :] = gram[0:half]
        own_ref[i, half:rows, :] = cross[0:half]
        other_ref[i, 0:half, :] = pltpu.roll(gram[half:rows], half, 1)
        other_ref[i, half:rows, :] = pltpu.roll(cross[half:rows], half, 1)


def local_ids(ids_ref, place, k):
    chip = lax.rem(lax.div(place, 2) + 4 - k, 4)
    ids = ids_ref[pl.ds(chip, 1), :]
    return jnp.where(lax.rem(place, 2) == 1, pltpu.roll(ids, 64, 1), ids)


def local_members(place, k, rows):
    chip = lax.rem(lax.div(place, 2) + 4 - k, 4)
    lane = lax.broadcasted_iota(jnp.int32, (rows, 128), 1)
    return chip * 128 + lax.rem(lane + 64 * lax.rem(place, 2), 128)


def begin_kernel(place_ref, ids_ref, own_ref, other_ref, inverse_ref, upper_ref, row_ref, m_ref):
    half, block = 64, 128
    place = place_ref[0]
    members = place * half + lax.broadcasted_iota(jnp.int32, (half, block), 0)
    for i in range(4):
        match = (local_ids(ids_ref, place, i) == members).astype(F32)
        m_ref[:, i * block : (i + 1) * block] = own_ref[i, half:block, :] + match

    def piece(i):
        return jnp.concatenate([own_ref[i, 0:half, :], pltpu.roll(other_ref[i], half, 1)], axis=0)

    inverse = invert_block(piece(0) + unit_block(block, block))
    inverse_ref[...] = inverse
    for i in range(1, 4):
        row_ref[:, (i - 1) * block : i * block] = piece(i)
    upper = dot_nn(inverse, row_ref[...], EXACT)
    upper_ref[...] = upper
    m_ref[:, block:] = m_ref[:, block:] - dot_nn(m_ref[:, :block], upper, EXACT)


def solve_kernel(
    place_ref, ids_ref, inverse_ref, upper_ref, row_ref, right_ref,
    g1_ref, g2_ref, g3_ref, h1_ref, h2_ref, h3_ref, out_ref, m_ref
):
    size, block, half = 512, 128, 64
    place = place_ref[0]
    unit = unit_block(block, block)

    def piece(mine, other, i):
        return jnp.concatenate([mine[i], pltpu.roll(other[i], half, 1)], axis=0)

    upper = upper_ref[...]
    row = row_ref[...]
    m_ref[...] = right_ref[...]
    a = {
        (1, 1): piece(g1_ref, h1_ref, 0) + unit,
        (1, 2): piece(g1_ref, h1_ref, 1),
        (2, 2): piece(g2_ref, h2_ref, 0) + unit,
        (2, 3): piece(g2_ref, h2_ref, 1),
        (3, 3): piece(g3_ref, h3_ref, 0) + unit,
        (1, 3): piece(g3_ref, h3_ref, 1).T,
    }
    inverses, uppers = {0: inverse_ref[...]}, {0: upper}
    for b in range(4):
        hi = (b + 1) * block
        if b:
            inverses[b] = invert_block(a[b, b])
            if hi < size:
                row = jnp.concatenate([a[b, j] for j in range(b + 1, 4)], axis=1)
                upper = dot_nn(inverses[b], row, EXACT)
                uppers[b] = upper
                m_ref[:, hi:] = m_ref[:, hi:] - dot_nn(m_ref[:, hi - block : hi], upper, EXACT)
        for i in range(b + 1, 4):
            left = row[:, (i - b - 1) * block : (i - b) * block]
            change = dot_tn(left, upper[:, (i - b - 1) * block :], EXACT)
            for j in range(i, 4):
                a[i, j] = a[i, j] - change[:, (j - i) * block : (j - i + 1) * block]
    for b in range(3, -1, -1):
        lo, hi = b * block, (b + 1) * block
        z = dot_nn(m_ref[:, lo:hi], inverses[b], EXACT)
        if hi < size:
            z = z - dot_nt(m_ref[:, hi:size], uppers[b], EXACT)
        m_ref[:, lo:hi] = z

    columns = jnp.concatenate(
        [jnp.broadcast_to(local_ids(ids_ref, place, k), (block, block)).T for k in range(4)], axis=0
    )
    own = place * half + lax.broadcasted_iota(jnp.int32, (half, block), 0)
    for k in range(4):
        match = (columns == local_members(place, k, size)).astype(F32)
        ordered = dot_nn(m_ref[...], match, EXACT)
        own_unit = (own == local_members(place, k, half)).astype(F32)
        out_ref[:, k * block : (k + 1) * block] = (ordered - own_unit).astype(BF16)


def update_kernel(t_ref, *rest):
    refs, out_ref = rest[:-1], rest[-1]
    members = t_ref.shape[1]
    mean = tree_sum([jnp.sum(ref[...].astype(F32), axis=0, keepdims=True) for ref in refs]) / members
    anomaly = jnp.concatenate([(ref[...].astype(F32) - mean).astype(BF16) for ref in refs], axis=0)
    increment = dot_nn(t_ref[...], anomaly)
    out_ref[...] = (refs[0][...].astype(F32) + increment).astype(BF16)


def body(members_field, predicted, noise, observed, obs_precision, obs_block, block_error_scale, member_ids):
    rows, width = predicted.shape
    members = member_ids.shape[0]
    cells = members_field.shape[1]
    half = width // 2
    factor = float(1.0 / (members - 1) ** 0.5)
    place = lax.axis_index("ens").reshape(1).astype(jnp.int32)
    swap = [(i, i ^ 1) for i in range(8)]
    smem = pl.BlockSpec(memory_space=pltpu.SMEM)
    vmem = pl.BlockSpec(memory_space=pltpu.VMEM)
    params = pltpu.CompilerParams(vmem_limit_bytes=32 * MIB)

    def shaped(*shape, dtype=F32):
        return jax.ShapeDtypeStruct(shape, dtype)

    def turned(array, steps):
        return lax.ppermute(array, "ens", [(i, (i + 2 * steps) % 8) for i in range(8)])

    def swapped(array):
        return lax.ppermute(array, "ens", swap)

    pred_got = swapped(predicted)
    noise_got = swapped(noise)
    facts = jnp.stack([obs_precision, observed, obs_block.astype(F32)])
    payload, side = pl.pallas_call(
        functools.partial(prepare_kernel, factor=factor),
        out_shape=(shaped(2 * rows + 16, half, dtype=BF16), shaped(8, half)),
        in_specs=[smem, smem, vmem, vmem, vmem],
        compiler_params=params,
        name="prepare",
    )(place, block_error_scale, predicted, pred_got, facts)
    payloads = [payload] + [turned(payload, k) for k in (1, 2, 3)]

    after_spread = lax.optimization_barrier((members_field, *payloads))
    field, payloads = after_spread[0], after_spread[1:]
    back, ahead = turned(field, 1), turned(field, 3)

    own, other = pl.pallas_call(
        functools.partial(gram_kernel, factor=factor),
        out_shape=(shaped(4, 2 * rows, 2 * rows),) * 2,
        in_specs=[smem] + [vmem] * 7,
        compiler_params=params,
        name="gram",
    )(place, *payloads, noise, noise_got, side)
    part = own + swapped(other)

    spread_out = lax.all_to_all(part.reshape(32, 16, 128), "space", split_axis=0, concat_axis=0)
    summed = jnp.sum(spread_out, axis=0)
    summed, back, ahead = lax.optimization_barrier((summed, back, ahead))
    cut = rows // 2
    beyond = [turned(back[:cut], 1), turned(ahead[cut:], 3)]
    whole = lax.all_to_all(
        jnp.broadcast_to(summed[None], (32, 16, 128)), "space", split_axis=0, concat_axis=0
    ).reshape(4, 2 * rows, 2 * rows)

    whole, *beyond = lax.optimization_barrier((whole, *beyond))
    gram = whole[:, :rows]
    near = gram[0:2]
    far = jnp.stack([gram[0], gram[2]])
    grams = [turned(near, 1), turned(near, 2), turned(far, 3)]
    ids = member_ids.reshape(4, 128)
    inverse, upper, row, right = pl.pallas_call(
        begin_kernel,
        out_shape=(shaped(128, 128), shaped(128, 384), shaped(128, 384), shaped(rows, members)),
        in_specs=[smem] + [vmem] * 3,
        compiler_params=params,
        name="begin",
    )(place, ids, whole, swapped(gram))
    inverse, *grams = lax.optimization_barrier((inverse, *grams))
    grams = grams + [swapped(g) for g in grams]
    inverse, *ready = lax.optimization_barrier((inverse, *grams, field, back, *beyond, ahead))
    grams, shares = ready[:6], ready[6:]
    others = [swapped(f) for f in shares]
    transform = pl.pallas_call(
        solve_kernel,
        out_shape=shaped(rows, members, dtype=BF16),
        in_specs=[smem] + [vmem] * 11,
        scratch_shapes=[pltpu.VMEM((rows, members), F32)],
        compiler_params=params,
        name="solve",
    )(place, ids, inverse, upper, row, right, *grams)

    pieces = [field, others[0], back, others[1], *shares[2:4], *others[2:4], ahead, others[4]]
    wide = 1024
    strips = [pl.BlockSpec((piece.shape[0], wide), lambda i: (0, i)) for piece in pieces]
    return pl.pallas_call(
        update_kernel,
        grid=(cells // wide,),
        out_shape=shaped(rows, cells, dtype=BF16),
        in_specs=[pl.BlockSpec((rows, members), lambda i: (0, 0))] + strips,
        out_specs=strips[0],
        compiler_params=params,
        name="update",
    )(transform, *pieces)


def solution(mesh):
    placed = (
        P("ens", "space"),
        P("ens", "space"),
        P("ens", "space"),
        P("space"),
        P("space"),
        P("space"),
        P(),
        P(),
    )
    return jax.shard_map(
        body, mesh=mesh, in_specs=placed, out_specs=P("ens", "space"), check_vma=False
    )
```

```python
import functools
import jax
import jax.numpy as jnp
from jax import lax
from jax.experimental import pallas as pl
from jax.experimental.pallas import tpu as pltpu
from jax.sharding import PartitionSpec as P

F32 = jnp.float32
BF16 = jnp.bfloat16
EXACT = lax.Precision.HIGHEST
MIB = 1024 * 1024


def across_rows(tile, row):
    return jnp.broadcast_to(tile[row : row + 1, :], tile.shape)


def across_lanes(tile, lane):
    return jnp.broadcast_to(tile[:, lane : lane + 1], tile.shape)


def dot_nt(a, b, precision=None):
    return lax.dot_general(
        a, b, (((1,), (1,)), ((), ())), precision=precision, preferred_element_type=F32
    )


def dot_tn(a, b, precision=None):
    return lax.dot_general(
        a, b, (((0,), (0,)), ((), ())), precision=precision, preferred_element_type=F32
    )


def dot_nn(a, b, precision=None):
    return jnp.dot(a, b, precision=precision, preferred_element_type=F32)


def tree_sum(terms):
    while len(terms) > 1:
        terms = [terms[i] + terms[i + 1] if i + 1 < len(terms) else terms[i] for i in range(0, len(terms), 2)]
    return terms[0]


def unit_block(rows, cols):
    at = lax.broadcasted_iota(jnp.int32, (rows, cols), 0)
    return (at == lax.broadcasted_iota(jnp.int32, (rows, cols), 1)).astype(F32)


def invert_block(block, beside=None):
    lanes = lax.broadcasted_iota(jnp.int32, (8, 128), 1)
    subs = lax.broadcasted_iota(jnp.int32, (8, 128), 0)
    tiles = [block[8 * i : 8 * i + 8, :] for i in range(16)]
    for t in range(16):
        old = tiles[t]
        cols = [across_lanes(old, 8 * t + j) for j in range(8)]
        panel = (lanes >= 8 * t) & (lanes < 8 * t + 8)
        old = jnp.where(panel, (lanes - 8 * t == subs).astype(F32), old)
        olds = [across_rows(old, j) for j in range(8)]
        for k in range(8):
            recip = 1.0 / across_rows(cols[k], k)
            pivot = cols[k]
            here = subs == k
            for j in range(8):
                if j != k:
                    scaled = across_rows(cols[j], k) * recip
                    cols[j] = jnp.where(here, scaled, cols[j] - pivot * scaled)
            cols[k] = jnp.where(here, recip, -pivot * recip)
        row = tree_sum([cols[j] * olds[j] for j in range(8)])
        rows = [across_rows(row, j) for j in range(8)]
        for i in [(t + 1 + n) % 16 for n in range(15)]:
            total = tree_sum([across_lanes(tiles[i], 8 * t + j) * rows[j] for j in range(8)])
            tiles[i] = jnp.where(panel, 0.0, tiles[i]) - total
        tiles[t] = row
        if beside is not None:
            beside(t)
    return jnp.concatenate(tiles, axis=0)


def prepare_kernel(place_ref, table_ref, facts_ref, mine_ref, got_ref, out_ref, side_ref, *, factor):
    half = mine_ref.shape[0]
    rows = 2 * half
    width = out_ref.shape[1]
    core = lax.rem(place_ref[0], 2)
    here = pl.ds(pl.multiple_of(core * width, 128), width)

    def line(which):
        count = width // 128
        return jnp.concatenate([facts_ref[which, pl.ds(core * count + j, 1), :] for j in range(count)], axis=1)

    block = line(2)
    error_scale = jnp.zeros_like(block)
    for b in range(32):
        level = jnp.broadcast_to(table_ref[:, b : b + 1], block.shape)
        error_scale = jnp.where(block == float(b), level, error_scale)
    scale = line(0) / error_scale * factor
    side_ref[...] = jnp.concatenate([scale, line(1), jnp.zeros((6, width), F32)], axis=0)
    mine = mine_ref[...]
    got = got_ref[:, here]
    mean = (jnp.sum(mine, axis=0, keepdims=True) + jnp.sum(got, axis=0, keepdims=True)) / rows
    out_ref[0:half, :] = ((mine - mean) * scale).astype(BF16)
    out_ref[half:rows, :] = ((got - mean) * scale).astype(BF16)
    high = mean.astype(BF16)
    rest = mean - high.astype(F32)
    mid = rest.astype(BF16)
    low = (rest - mid.astype(F32)).astype(BF16)
    out_ref[rows : rows + 16, :] = jnp.concatenate([high, mid, low, jnp.zeros((13, width), BF16)], axis=0)


def gram_kernel(
    place_ref, p0_ref, p1_ref, p2_ref, p3_ref, mine_ref, got_ref, side_ref, own_ref, other_ref, *, factor
):
    refs = (p0_ref, p1_ref, p2_ref, p3_ref)
    rows = p0_ref.shape[0] - 16
    half = rows // 2
    width = p0_ref.shape[1]
    here = pl.ds(pl.multiple_of(lax.rem(place_ref[0], 2) * width, 128), width)
    scale = side_ref[0:1, :]
    means = []
    for ref in refs:
        tail = ref[rows : rows + 16, :].astype(F32)
        means.append(tail[0:1, :] + (tail[1:2, :] + tail[2:3, :]))
    mean = ((means[0] + means[1]) + (means[2] + means[3])) * 0.25
    spreads = [
        (ref[0:rows, :].astype(F32) + scale * (m - mean)).astype(BF16) for ref, m in zip(refs, means)
    ]
    left_over = tree_sum([jnp.sum(s.astype(F32), axis=0, keepdims=True) for s in spreads]) / (4 * rows)
    over_high = left_over.astype(BF16)
    over_low = (left_over - over_high.astype(F32)).astype(BF16)
    over = jnp.concatenate([over_high, over_low, jnp.zeros((14, width), BF16)], axis=0)
    shift = scale * (side_ref[1:2, :] - mean)
    noise = jnp.concatenate([mine_ref[...], got_ref[:, here]], axis=0)
    right = shift + factor * noise
    high = right.astype(BF16)
    low = (right - high.astype(F32)).astype(BF16)
    left = jnp.concatenate([spreads[0], high, low, over], axis=0)
    at_over = dot_nt(left, over)
    at_over = at_over[:, 0:1] + at_over[:, 1:2]
    gram_over = at_over[0:rows]
    cross_over = at_over[rows : 2 * rows] + at_over[2 * rows : 3 * rows]
    both = at_over[3 * rows : 3 * rows + 1] + at_over[3 * rows + 1 : 3 * rows + 2]
    for i in range(4):
        part = dot_nt(left, spreads[i])
        over_row = part[3 * rows : 3 * rows + 1] + part[3 * rows + 1 : 3 * rows + 2]
        gram = part[0:rows] - gram_over - (over_row - both)
        cross = part[rows : 2 * rows] + part[2 * rows : 3 * rows] - cross_over
        own_ref[i, 0:half, :] = gram[0:half]
        own_ref[i, half:rows, :] = cross[0:half]
        other_ref[i, 0:half, :] = pltpu.roll(gram[half:rows], half, 1)
        other_ref[i, half:rows, :] = pltpu.roll(cross[half:rows], half, 1)


def local_ids(ids_ref, place, k):
    chip = lax.rem(lax.div(place, 2) + 4 - k, 4)
    ids = ids_ref[pl.ds(chip, 1), :]
    return jnp.where(lax.rem(place, 2) == 1, pltpu.roll(ids, 64, 1), ids)


def local_members(place, k, rows):
    chip = lax.rem(lax.div(place, 2) + 4 - k, 4)
    lane = lax.broadcasted_iota(jnp.int32, (rows, 128), 1)
    return chip * 128 + lax.rem(lane + 64 * lax.rem(place, 2), 128)


def begin_kernel(place_ref, ids_ref, own_ref, other_ref, inverse_ref, upper_ref, row_ref, m_ref):
    half, block = 64, 128
    place = place_ref[0]
    def piece(i):
        return jnp.concatenate([own_ref[i, 0:half, :], pltpu.roll(other_ref[i], half, 1)], axis=0)

    inverse = invert_block(piece(0) + unit_block(block, block))
    inverse_ref[...] = inverse
    for i in range(1, 4):
        row_ref[:, (i - 1) * block : i * block] = piece(i)
    upper = dot_nn(inverse, row_ref[...], EXACT)
    upper_ref[...] = upper
    members = place * half + lax.broadcasted_iota(jnp.int32, (half, block), 0)
    for i in range(4):
        match = (local_ids(ids_ref, place, i) == members.astype(F32)).astype(F32)
        m_ref[:, i * block : (i + 1) * block] = own_ref[i, half:block, :] + match
    m_ref[:, block:] = m_ref[:, block:] - dot_nn(m_ref[:, :block], upper, EXACT)


def solve_kernel(
    place_ref, ids_ref, inverse_ref, upper_ref, row_ref, right_ref,
    g1_ref, g2_ref, g3_ref, theirs_ref, *rest
):
    fields, (out_ref, anomaly_ref, m_ref) = rest[:-3], rest[-3:]
    size, block, half = 512, 128, 64
    place = place_ref[0]
    unit = unit_block(block, block)

    def piece(mine, k, i):
        return jnp.concatenate([mine[i], pltpu.roll(theirs_ref[2 * (k - 1) + i], half, 1)], axis=0)

    def centre(strip):
        here = slice(strip * block, (strip + 1) * block)
        sums = [jnp.sum(ref[:, here].astype(F32), axis=0, keepdims=True) for ref in fields]
        mean = tree_sum(sums) / size
        at = 0
        for ref in fields:
            anomaly_ref[at : at + ref.shape[0], here] = (ref[:, here].astype(F32) - mean).astype(BF16)
            at += ref.shape[0]

    strips = anomaly_ref.shape[1] // block

    def beside(b, t):
        step = (b - 1) * 16 + t
        for strip in range(step * strips // 48, (step + 1) * strips // 48):
            centre(strip)

    upper = upper_ref[...]
    row = row_ref[...]
    m_ref[...] = right_ref[...]
    a = {
        (1, 1): piece(g1_ref, 1, 0) + unit,
        (1, 2): piece(g1_ref, 1, 1),
        (2, 2): piece(g2_ref, 2, 0) + unit,
        (2, 3): piece(g2_ref, 2, 1),
        (3, 3): piece(g3_ref, 3, 0) + unit,
        (1, 3): piece(g3_ref, 3, 1).T,
    }
    inverses, uppers = {0: inverse_ref[...]}, {0: upper}
    for b in range(4):
        hi = (b + 1) * block
        if b:
            inverses[b] = invert_block(a[b, b], functools.partial(beside, b))
            if hi < size:
                row = jnp.concatenate([a[b, j] for j in range(b + 1, 4)], axis=1)
                upper = dot_nn(inverses[b], row, EXACT)
                uppers[b] = upper
                m_ref[:, hi:] = m_ref[:, hi:] - dot_nn(m_ref[:, hi - block : hi], upper, EXACT)
        for i in range(b + 1, 4):
            left = row[:, (i - b - 1) * block : (i - b) * block]
            change = dot_tn(left, upper[:, (i - b - 1) * block :], EXACT)
            for j in range(i, 4):
                a[i, j] = a[i, j] - change[:, (j - i) * block : (j - i + 1) * block]
    for b in range(3, -1, -1):
        lo, hi = b * block, (b + 1) * block
        z = dot_nn(m_ref[:, lo:hi], inverses[b], EXACT)
        if hi < size:
            z = z - dot_nt(m_ref[:, hi:size], uppers[b], EXACT)
        m_ref[:, lo:hi] = z

    columns = jnp.concatenate(
        [jnp.broadcast_to(local_ids(ids_ref, place, k), (block, block)).T for k in range(4)], axis=0
    )
    own = place * half + lax.broadcasted_iota(jnp.int32, (half, block), 0)
    for k in range(4):
        match = (columns == local_members(place, k, size).astype(F32)).astype(F32)
        ordered = dot_nn(m_ref[...], match, EXACT)
        own_unit = (own == local_members(place, k, half)).astype(F32)
        out_ref[:, k * block : (k + 1) * block] = (ordered - own_unit).astype(BF16)


def update_kernel(t_ref, field_ref, anomaly_ref, out_ref):
    wide = 1024
    for at in range(0, out_ref.shape[1], wide):
        here = slice(at, at + wide)
        increment = dot_nn(t_ref[...], anomaly_ref[:, here])
        out_ref[:, here] = (field_ref[:, here].astype(F32) + increment).astype(BF16)


def body(members_field, predicted, noise, observed, obs_precision, obs_block, block_error_scale, member_ids):
    rows, width = predicted.shape
    members = member_ids.shape[0]
    cells = members_field.shape[1]
    half = width // 2
    factor = float(1.0 / (members - 1) ** 0.5)
    place = lax.axis_index("ens").reshape(1).astype(jnp.int32)
    swap = [(i, i ^ 1) for i in range(8)]
    smem = pl.BlockSpec(memory_space=pltpu.SMEM)
    vmem = pl.BlockSpec(memory_space=pltpu.VMEM)

    def room(mib):
        return pltpu.CompilerParams(vmem_limit_bytes=mib * MIB)

    def shaped(*shape, dtype=F32):
        return jax.ShapeDtypeStruct(shape, dtype)

    def turned(array, steps):
        return lax.ppermute(array, "ens", [(i, (i + 2 * steps) % 8) for i in range(8)])

    def swapped(array):
        return lax.ppermute(array, "ens", swap)

    pred_got = swapped(predicted)
    core = lax.rem(lax.axis_index("ens"), 2)
    pred_mine = lax.dynamic_slice_in_dim(predicted, core * half, half, 1)
    noise_mine = lax.dynamic_slice_in_dim(noise, core * half, half, 1)
    facts = jnp.stack([a.reshape(-1, 128).astype(F32) for a in (obs_precision, observed, obs_block)])
    table = jnp.pad(block_error_scale, (0, 128 - block_error_scale.shape[0])).reshape(1, 128)
    payload, side = pl.pallas_call(
        functools.partial(prepare_kernel, factor=factor),
        out_shape=(shaped(2 * rows + 16, half, dtype=BF16), shaped(8, half)),
        in_specs=[smem] + [vmem] * 4,
        compiler_params=room(32),
        name="prepare",
    )(place, table, facts, pred_mine, pred_got)
    payload, noise_after = lax.optimization_barrier((payload, noise))
    noise_got = swapped(noise_after)
    payloads = [payload] + [turned(payload, k) for k in (1, 2, 3)]

    ids = member_ids.astype(F32).reshape(4, 128)
    after_spread = lax.optimization_barrier((members_field, noise_mine, ids, *payloads))
    (field, noise_mine, ids), payloads = after_spread[:3], after_spread[3:]
    back, ahead = turned(field, 1), turned(field, 3)

    own, other = pl.pallas_call(
        functools.partial(gram_kernel, factor=factor),
        out_shape=(shaped(4, 2 * rows, 2 * rows),) * 2,
        in_specs=[smem] + [vmem] * 7,
        compiler_params=room(8),
        name="gram",
    )(place, *payloads, noise_mine, noise_got, side)
    part = own + swapped(other)

    spread_out = lax.all_to_all(part.reshape(32, 16, 128), "space", split_axis=0, concat_axis=0)
    summed = jnp.sum(spread_out, axis=0)
    summed, back, ahead, near_field = lax.optimization_barrier((summed, back, ahead, field))
    cut = rows // 2
    beyond = [turned(back[:cut], 1), turned(ahead[cut:], 3)]
    others = [swapped(back), swapped(ahead), swapped(near_field)]
    whole = lax.all_to_all(
        jnp.broadcast_to(summed[None], (32, 16, 128)), "space", split_axis=0, concat_axis=0
    ).reshape(4, 2 * rows, 2 * rows)

    whole, *moved = lax.optimization_barrier((whole, *beyond, *others))
    beyond, others = moved[:2], moved[2:]
    gram = whole[:, :rows]
    near = gram[0:2]
    far = jnp.stack([gram[0], gram[2]])
    grams = [turned(near, 1), turned(near, 2), turned(far, 3)]
    gram_other = swapped(gram)
    inverse, upper, row, right = pl.pallas_call(
        begin_kernel,
        out_shape=(
            shaped(128, 128),
            shaped(128, 384),
            shaped(128, 384),
            shaped(rows, members),
        ),
        in_specs=[smem, vmem, vmem, vmem],
        compiler_params=room(8),
        name="begin",
    )(place, ids, whole, gram_other)
    inverse, *after = lax.optimization_barrier((inverse, *grams, *beyond))
    grams, beyond = after[:3], after[3:]
    beyond_others = [swapped(f) for f in beyond]
    theirs = swapped(jnp.concatenate(grams, axis=0))
    fields = [field, others[2], back, others[0], *beyond, *beyond_others, ahead, others[1]]
    transform, anomaly = pl.pallas_call(
        solve_kernel,
        out_shape=(shaped(rows, members, dtype=BF16), shaped(members, cells, dtype=BF16)),
        in_specs=[smem] + [vmem] * (9 + len(fields)),
        scratch_shapes=[pltpu.VMEM((rows, members), F32)],
        compiler_params=room(22),
        name="solve",
    )(place, ids, inverse, upper, row, right, *grams, theirs, *fields)
    return pl.pallas_call(
        update_kernel,
        out_shape=shaped(rows, cells, dtype=BF16),
        in_specs=[vmem] * 3,
        compiler_params=room(14),
        name="update",
    )(transform, field, anomaly)


def solution(mesh):
    placed = (
        P("ens", "space"),
        P("ens", "space"),
        P("ens", "space"),
        P("space"),
        P("space"),
        P("space"),
        P(),
        P(),
    )
    return jax.shard_map(
        body, mesh=mesh, in_specs=placed, out_specs=P("ens", "space"), check_vma=False
    )
```

```python
import functools
import jax
import jax.numpy as jnp
from jax import lax
from jax.experimental import pallas as pl
from jax.experimental.pallas import tpu as pltpu
from jax.sharding import PartitionSpec as P

F32 = jnp.float32
BF16 = jnp.bfloat16
EXACT = lax.Precision.HIGHEST
MIB = 1024 * 1024


def across_rows(tile, row):
    return jnp.broadcast_to(tile[row : row + 1, :], tile.shape)


def across_lanes(tile, lane):
    return jnp.broadcast_to(tile[:, lane : lane + 1], tile.shape)


def dot_nt(a, b, precision=None):
    return lax.dot_general(
        a, b, (((1,), (1,)), ((), ())), precision=precision, preferred_element_type=F32
    )


def dot_tn(a, b, precision=None):
    return lax.dot_general(
        a, b, (((0,), (0,)), ((), ())), precision=precision, preferred_element_type=F32
    )


def dot_nn(a, b, precision=None):
    return jnp.dot(a, b, precision=precision, preferred_element_type=F32)


def tree_sum(terms):
    while len(terms) > 1:
        terms = [terms[i] + terms[i + 1] if i + 1 < len(terms) else terms[i] for i in range(0, len(terms), 2)]
    return terms[0]


def unit_block(rows, cols):
    at = lax.broadcasted_iota(jnp.int32, (rows, cols), 0)
    return (at == lax.broadcasted_iota(jnp.int32, (rows, cols), 1)).astype(F32)


def invert_block(block, beside=None):
    lanes = lax.broadcasted_iota(jnp.int32, (8, 128), 1)
    subs = lax.broadcasted_iota(jnp.int32, (8, 128), 0)
    tiles = [block[8 * i : 8 * i + 8, :] for i in range(16)]
    for t in range(16):
        old = tiles[t]
        cols = [across_lanes(old, 8 * t + j) for j in range(8)]
        panel = (lanes >= 8 * t) & (lanes < 8 * t + 8)
        old = jnp.where(panel, (lanes - 8 * t == subs).astype(F32), old)
        olds = [across_rows(old, j) for j in range(8)]
        for k in range(8):
            recip = 1.0 / across_rows(cols[k], k)
            pivot = cols[k]
            here = subs == k
            for j in range(8):
                if j != k:
                    scaled = across_rows(cols[j], k) * recip
                    cols[j] = jnp.where(here, scaled, cols[j] - pivot * scaled)
            cols[k] = jnp.where(here, recip, -pivot * recip)
        row = tree_sum([cols[j] * olds[j] for j in range(8)])
        rows = [across_rows(row, j) for j in range(8)]
        for i in [(t + 1 + n) % 16 for n in range(15)]:
            total = tree_sum([across_lanes(tiles[i], 8 * t + j) * rows[j] for j in range(8)])
            tiles[i] = jnp.where(panel, 0.0, tiles[i]) - total
        tiles[t] = row
        if beside is not None:
            beside(t)
    return jnp.concatenate(tiles, axis=0)


def prepare_kernel(place_ref, mine_ref, got_ref, out_ref):
    half = mine_ref.shape[0]
    rows = 2 * half
    width = out_ref.shape[1]
    here = pl.ds(pl.multiple_of(lax.rem(place_ref[0], 2) * width, 128), width)
    mine = mine_ref[...]
    got = got_ref[:, here]
    mean = (jnp.sum(mine, axis=0, keepdims=True) + jnp.sum(got, axis=0, keepdims=True)) / rows
    out_ref[0:half, :] = (mine - mean).astype(BF16)
    out_ref[half:rows, :] = (got - mean).astype(BF16)
    high = mean.astype(BF16)
    rest = mean - high.astype(F32)
    mid = rest.astype(BF16)
    low = (rest - mid.astype(F32)).astype(BF16)
    out_ref[rows : rows + 16, :] = jnp.concatenate([high, mid, low, jnp.zeros((13, width), BF16)], axis=0)


def gram_kernel(
    place_ref, p0_ref, p1_ref, p2_ref, p3_ref, mine_ref, got_ref, facts_ref, table_ref, own_ref, other_ref, *, factor
):
    refs = (p0_ref, p1_ref, p2_ref, p3_ref)
    rows = p0_ref.shape[0] - 16
    half = rows // 2
    width = p0_ref.shape[1]
    core = lax.rem(place_ref[0], 2)
    here = pl.ds(pl.multiple_of(core * width, 128), width)

    def line(which):
        count = width // 128
        return jnp.concatenate([facts_ref[which, pl.ds(core * count + j, 1), :] for j in range(count)], axis=1)

    block = line(2)
    error_scale = jnp.zeros_like(block)
    for b in range(32):
        level = jnp.broadcast_to(table_ref[:, b : b + 1], block.shape)
        error_scale = jnp.where(block == float(b), level, error_scale)
    scale = line(0) / error_scale * factor
    means = []
    for ref in refs:
        tail = ref[rows : rows + 16, :].astype(F32)
        means.append(tail[0:1, :] + (tail[1:2, :] + tail[2:3, :]))
    mean = ((means[0] + means[1]) + (means[2] + means[3])) * 0.25
    spreads = [
        (scale * (ref[0:rows, :].astype(F32) + (m - mean))).astype(BF16) for ref, m in zip(refs, means)
    ]
    left_over = tree_sum([jnp.sum(s.astype(F32), axis=0, keepdims=True) for s in spreads]) / (4 * rows)
    over_high = left_over.astype(BF16)
    over_low = (left_over - over_high.astype(F32)).astype(BF16)
    over = jnp.concatenate([over_high, over_low, jnp.zeros((14, width), BF16)], axis=0)
    shift = scale * (line(1) - mean)
    noise = jnp.concatenate([mine_ref[...], got_ref[:, here]], axis=0)
    right = shift + factor * noise
    high = right.astype(BF16)
    low = (right - high.astype(F32)).astype(BF16)
    left = jnp.concatenate([spreads[0], high, low, over], axis=0)
    at_over = dot_nt(left, over)
    at_over = at_over[:, 0:1] + at_over[:, 1:2]
    gram_over = at_over[0:rows]
    cross_over = at_over[rows : 2 * rows] + at_over[2 * rows : 3 * rows]
    both = at_over[3 * rows : 3 * rows + 1] + at_over[3 * rows + 1 : 3 * rows + 2]
    for i in range(4):
        part = dot_nt(left, spreads[i])
        over_row = part[3 * rows : 3 * rows + 1] + part[3 * rows + 1 : 3 * rows + 2]
        gram = part[0:rows] - gram_over - (over_row - both)
        cross = part[rows : 2 * rows] + part[2 * rows : 3 * rows] - cross_over
        own_ref[i, 0:half, :] = gram[0:half]
        own_ref[i, half:rows, :] = cross[0:half]
        other_ref[i, 0:half, :] = pltpu.roll(gram[half:rows], half, 1)
        other_ref[i, half:rows, :] = pltpu.roll(cross[half:rows], half, 1)


def local_ids(ids_ref, place, k):
    chip = lax.rem(lax.div(place, 2) + 4 - k, 4)
    ids = ids_ref[pl.ds(chip, 1), :]
    return jnp.where(lax.rem(place, 2) == 1, pltpu.roll(ids, 64, 1), ids)


def local_members(place, k, rows):
    chip = lax.rem(lax.div(place, 2) + 4 - k, 4)
    lane = lax.broadcasted_iota(jnp.int32, (rows, 128), 1)
    return chip * 128 + lax.rem(lane + 64 * lax.rem(place, 2), 128)


def begin_kernel(place_ref, ids_ref, own_ref, other_ref, inverse_ref, upper_ref, row_ref, m_ref):
    half, block = 64, 128
    place = place_ref[0]
    def piece(i):
        return jnp.concatenate([own_ref[i, 0:half, :], pltpu.roll(other_ref[i], half, 1)], axis=0)

    inverse = invert_block(piece(0) + unit_block(block, block))
    inverse_ref[...] = inverse
    for i in range(1, 4):
        row_ref[:, (i - 1) * block : i * block] = piece(i)
    upper = dot_nn(inverse, row_ref[...], EXACT)
    upper_ref[...] = upper
    members = place * half + lax.broadcasted_iota(jnp.int32, (half, block), 0)
    for i in range(4):
        match = (local_ids(ids_ref, place, i) == members.astype(F32)).astype(F32)
        m_ref[:, i * block : (i + 1) * block] = own_ref[i, half:block, :] + match
    m_ref[:, block:] = m_ref[:, block:] - dot_nn(m_ref[:, :block], upper, EXACT)


def solve_kernel(
    place_ref, ids_ref, inverse_ref, upper_ref, row_ref, right_ref,
    g1_ref, g2_ref, g3_ref, theirs_ref, *rest
):
    fields, (out_ref, anomaly_ref, m_ref) = rest[:-3], rest[-3:]
    size, block, half = 512, 128, 64
    place = place_ref[0]
    unit = unit_block(block, block)

    def piece(mine, k, i):
        return jnp.concatenate([mine[i], pltpu.roll(theirs_ref[2 * (k - 1) + i], half, 1)], axis=0)

    def centre(strip):
        here = slice(strip * block, (strip + 1) * block)
        sums = [jnp.sum(ref[:, here].astype(F32), axis=0, keepdims=True) for ref in fields]
        mean = tree_sum(sums) / size
        at = 0
        for ref in fields:
            anomaly_ref[at : at + ref.shape[0], here] = (ref[:, here].astype(F32) - mean).astype(BF16)
            at += ref.shape[0]

    strips = anomaly_ref.shape[1] // block

    def beside(b, t):
        step = (b - 1) * 16 + t
        for strip in range(step * strips // 48, (step + 1) * strips // 48):
            centre(strip)

    upper = upper_ref[...]
    row = row_ref[...]
    m_ref[...] = right_ref[...]
    a = {
        (1, 1): piece(g1_ref, 1, 0) + unit,
        (1, 2): piece(g1_ref, 1, 1),
        (2, 2): piece(g2_ref, 2, 0) + unit,
        (2, 3): piece(g2_ref, 2, 1),
        (3, 3): piece(g3_ref, 3, 0) + unit,
        (1, 3): piece(g3_ref, 3, 1).T,
    }
    inverses, uppers = {0: inverse_ref[...]}, {0: upper}
    for b in range(4):
        hi = (b + 1) * block
        if b:
            inverses[b] = invert_block(a[b, b], functools.partial(beside, b))
            if hi < size:
                row = jnp.concatenate([a[b, j] for j in range(b + 1, 4)], axis=1)
                upper = dot_nn(inverses[b], row, EXACT)
                uppers[b] = upper
                m_ref[:, hi:] = m_ref[:, hi:] - dot_nn(m_ref[:, hi - block : hi], upper, EXACT)
        for i in range(b + 1, 4):
            left = row[:, (i - b - 1) * block : (i - b) * block]
            change = dot_tn(left, upper[:, (i - b - 1) * block :], EXACT)
            for j in range(i, 4):
                a[i, j] = a[i, j] - change[:, (j - i) * block : (j - i + 1) * block]
    for b in range(3, -1, -1):
        lo, hi = b * block, (b + 1) * block
        z = dot_nn(m_ref[:, lo:hi], inverses[b], EXACT)
        if hi < size:
            z = z - dot_nt(m_ref[:, hi:size], uppers[b], EXACT)
        m_ref[:, lo:hi] = z

    columns = jnp.concatenate(
        [jnp.broadcast_to(local_ids(ids_ref, place, k), (block, block)).T for k in range(4)], axis=0
    )
    own = place * half + lax.broadcasted_iota(jnp.int32, (half, block), 0)
    for k in range(4):
        match = (columns == local_members(place, k, size).astype(F32)).astype(F32)
        ordered = dot_nn(m_ref[...], match, EXACT)
        own_unit = (own == local_members(place, k, half)).astype(F32)
        out_ref[:, k * block : (k + 1) * block] = (ordered - own_unit).astype(BF16)


def update_kernel(t_ref, field_ref, anomaly_ref, out_ref):
    wide = 1024
    for at in range(0, out_ref.shape[1], wide):
        here = slice(at, at + wide)
        increment = dot_nn(t_ref[...], anomaly_ref[:, here])
        out_ref[:, here] = (field_ref[:, here].astype(F32) + increment).astype(BF16)


def body(members_field, predicted, noise, observed, obs_precision, obs_block, block_error_scale, member_ids):
    rows, width = predicted.shape
    members = member_ids.shape[0]
    cells = members_field.shape[1]
    half = width // 2
    factor = float(1.0 / (members - 1) ** 0.5)
    place = lax.axis_index("ens").reshape(1).astype(jnp.int32)
    swap = [(i, i ^ 1) for i in range(8)]
    smem = pl.BlockSpec(memory_space=pltpu.SMEM)
    vmem = pl.BlockSpec(memory_space=pltpu.VMEM)

    def room(mib):
        return pltpu.CompilerParams(vmem_limit_bytes=mib * MIB)

    def shaped(*shape, dtype=F32):
        return jax.ShapeDtypeStruct(shape, dtype)

    def turned(array, steps):
        return lax.ppermute(array, "ens", [(i, (i + 2 * steps) % 8) for i in range(8)])

    def swapped(array):
        return lax.ppermute(array, "ens", swap)

    pred_got = swapped(predicted)
    core = lax.rem(lax.axis_index("ens"), 2)
    pred_mine = lax.dynamic_slice_in_dim(predicted, core * half, half, 1)
    payload = pl.pallas_call(
        prepare_kernel,
        out_shape=shaped(2 * rows + 16, half, dtype=BF16),
        in_specs=[smem, vmem, vmem],
        compiler_params=room(32),
        name="prepare",
    )(place, pred_mine, pred_got)
    payload, noise, member_ids, obs_precision, observed, obs_block, block_error_scale = lax.optimization_barrier(
        (payload, noise, member_ids, obs_precision, observed, obs_block, block_error_scale)
    )
    noise_got = swapped(noise)
    noise_mine = lax.dynamic_slice_in_dim(noise, core * half, half, 1)
    facts = jnp.stack([a.reshape(-1, 128).astype(F32) for a in (obs_precision, observed, obs_block)])
    table = jnp.pad(block_error_scale, (0, 128 - block_error_scale.shape[0])).reshape(1, 128)
    payloads = [payload] + [turned(payload, k) for k in (1, 2, 3)]

    ids = member_ids.astype(F32).reshape(4, 128)
    after_spread = lax.optimization_barrier((members_field, noise_mine, ids, facts, table, *payloads))
    (field, noise_mine, ids, facts, table), payloads = after_spread[:5], after_spread[5:]
    back, ahead = turned(field, 1), turned(field, 3)

    own, other = pl.pallas_call(
        functools.partial(gram_kernel, factor=factor),
        out_shape=(shaped(4, 2 * rows, 2 * rows),) * 2,
        in_specs=[smem] + [vmem] * 8,
        compiler_params=room(8),
        name="gram",
    )(place, *payloads, noise_mine, noise_got, facts, table)
    part = own + swapped(other)

    spread_out = lax.all_to_all(part.reshape(32, 16, 128), "space", split_axis=0, concat_axis=0)
    summed = jnp.sum(spread_out, axis=0)
    summed, back, ahead, near_field = lax.optimization_barrier((summed, back, ahead, field))
    cut = rows // 2
    beyond = [turned(back[:cut], 1), turned(ahead[cut:], 3)]
    others = [swapped(back), swapped(ahead), swapped(near_field)]
    whole = lax.all_to_all(
        jnp.broadcast_to(summed[None], (32, 16, 128)), "space", split_axis=0, concat_axis=0
    ).reshape(4, 2 * rows, 2 * rows)

    whole, *moved = lax.optimization_barrier((whole, *beyond, *others))
    beyond, others = moved[:2], moved[2:]
    gram = whole[:, :rows]
    near = gram[0:2]
    far = jnp.stack([gram[0], gram[2]])
    grams = [turned(near, 1), turned(near, 2), turned(far, 3)]
    gram_other = swapped(gram)
    inverse, upper, row, right = pl.pallas_call(
        begin_kernel,
        out_shape=(
            shaped(128, 128),
            shaped(128, 384),
            shaped(128, 384),
            shaped(rows, members),
        ),
        in_specs=[smem, vmem, vmem, vmem],
        compiler_params=room(8),
        name="begin",
    )(place, ids, whole, gram_other)
    inverse, *after = lax.optimization_barrier((inverse, *grams, *beyond))
    grams, beyond = after[:3], after[3:]
    beyond_others = [swapped(f) for f in beyond]
    theirs = swapped(jnp.concatenate(grams, axis=0))
    fields = [field, others[2], back, others[0], *beyond, *beyond_others, ahead, others[1]]
    transform, anomaly = pl.pallas_call(
        solve_kernel,
        out_shape=(shaped(rows, members, dtype=BF16), shaped(members, cells, dtype=BF16)),
        in_specs=[smem] + [vmem] * (9 + len(fields)),
        scratch_shapes=[pltpu.VMEM((rows, members), F32)],
        compiler_params=room(22),
        name="solve",
    )(place, ids, inverse, upper, row, right, *grams, theirs, *fields)
    return pl.pallas_call(
        update_kernel,
        out_shape=shaped(rows, cells, dtype=BF16),
        in_specs=[vmem] * 3,
        compiler_params=room(14),
        name="update",
    )(transform, field, anomaly)


def solution(mesh):
    placed = (
        P("ens", "space"),
        P("ens", "space"),
        P("ens", "space"),
        P("space"),
        P("space"),
        P("space"),
        P(),
        P(),
    )
    return jax.shard_map(
        body, mesh=mesh, in_specs=placed, out_specs=P("ens", "space"), check_vma=False
    )
```

```python
import functools
import jax
import jax.numpy as jnp
from jax import lax
from jax.experimental import pallas as pl
from jax.experimental.pallas import tpu as pltpu
from jax.sharding import PartitionSpec as P

F32 = jnp.float32
BF16 = jnp.bfloat16
EXACT = lax.Precision.HIGHEST
MIB = 1024 * 1024


def across_rows(tile, row):
    return jnp.broadcast_to(tile[row : row + 1, :], tile.shape)


def across_lanes(tile, lane):
    return jnp.broadcast_to(tile[:, lane : lane + 1], tile.shape)


def dot_nt(a, b, precision=None):
    return lax.dot_general(
        a, b, (((1,), (1,)), ((), ())), precision=precision, preferred_element_type=F32
    )


def dot_tn(a, b, precision=None):
    return lax.dot_general(
        a, b, (((0,), (0,)), ((), ())), precision=precision, preferred_element_type=F32
    )


def dot_nn(a, b, precision=None):
    return jnp.dot(a, b, precision=precision, preferred_element_type=F32)


def tree_sum(terms):
    while len(terms) > 1:
        terms = [terms[i] + terms[i + 1] if i + 1 < len(terms) else terms[i] for i in range(0, len(terms), 2)]
    return terms[0]


def unit_block(rows, cols):
    at = lax.broadcasted_iota(jnp.int32, (rows, cols), 0)
    return (at == lax.broadcasted_iota(jnp.int32, (rows, cols), 1)).astype(F32)


def invert_block(block, beside=None):
    lanes = lax.broadcasted_iota(jnp.int32, (8, 128), 1)
    subs = lax.broadcasted_iota(jnp.int32, (8, 128), 0)
    tiles = [block[8 * i : 8 * i + 8, :] for i in range(16)]
    for t in range(16):
        old = tiles[t]
        cols = [across_lanes(old, 8 * t + j) for j in range(8)]
        panel = (lanes >= 8 * t) & (lanes < 8 * t + 8)
        old = jnp.where(panel, (lanes - 8 * t == subs).astype(F32), old)
        olds = [across_rows(old, j) for j in range(8)]
        for k in range(8):
            recip = 1.0 / across_rows(cols[k], k)
            pivot = cols[k]
            here = subs == k
            for j in range(8):
                if j != k:
                    scaled = across_rows(cols[j], k) * recip
                    cols[j] = jnp.where(here, scaled, cols[j] - pivot * scaled)
            cols[k] = jnp.where(here, recip, -pivot * recip)
        row = tree_sum([cols[j] * olds[j] for j in range(8)])
        rows = [across_rows(row, j) for j in range(8)]
        for i in [(t + 1 + n) % 16 for n in range(15)]:
            total = tree_sum([across_lanes(tiles[i], 8 * t + j) * rows[j] for j in range(8)])
            tiles[i] = jnp.where(panel, 0.0, tiles[i]) - total
        tiles[t] = row
        if beside is not None:
            beside(t)
    return jnp.concatenate(tiles, axis=0)


def prepare_kernel(place_ref, mine_ref, got_ref, out_ref):
    half = mine_ref.shape[0]
    rows = 2 * half
    width = out_ref.shape[1]
    here = pl.ds(pl.multiple_of(lax.rem(place_ref[0], 2) * width, 128), width)
    mine = mine_ref[...]
    got = got_ref[:, here]
    mean = (jnp.sum(mine, axis=0, keepdims=True) + jnp.sum(got, axis=0, keepdims=True)) / rows
    out_ref[0:half, :] = (mine - mean).astype(BF16)
    out_ref[half:rows, :] = (got - mean).astype(BF16)
    high = mean.astype(BF16)
    rest = mean - high.astype(F32)
    mid = rest.astype(BF16)
    low = (rest - mid.astype(F32)).astype(BF16)
    out_ref[rows : rows + 16, :] = jnp.concatenate([high, mid, low, jnp.zeros((13, width), BF16)], axis=0)


def gram_kernel(
    place_ref, p0_ref, p1_ref, p2_ref, p3_ref, mine_ref, got_ref, facts_ref, table_ref, own_ref, other_ref, *, factor
):
    refs = (p0_ref, p1_ref, p2_ref, p3_ref)
    rows = p0_ref.shape[0] - 16
    half = rows // 2
    width = p0_ref.shape[1]
    core = lax.rem(place_ref[0], 2)
    here = pl.ds(pl.multiple_of(core * width, 128), width)

    def line(which):
        count = width // 128
        return jnp.concatenate([facts_ref[which, pl.ds(core * count + j, 1), :] for j in range(count)], axis=1)

    block = line(2)
    error_scale = jnp.zeros_like(block)
    for b in range(32):
        level = jnp.broadcast_to(table_ref[:, b : b + 1], block.shape)
        error_scale = jnp.where(block == float(b), level, error_scale)
    scale = line(0) / error_scale * factor
    means = []
    for ref in refs:
        tail = ref[rows : rows + 16, :].astype(F32)
        means.append(tail[0:1, :] + (tail[1:2, :] + tail[2:3, :]))
    mean = ((means[0] + means[1]) + (means[2] + means[3])) * 0.25
    spreads = [
        (scale * (ref[0:rows, :].astype(F32) + (m - mean))).astype(BF16) for ref, m in zip(refs, means)
    ]
    left_over = tree_sum([jnp.sum(s.astype(F32), axis=0, keepdims=True) for s in spreads]) / (4 * rows)
    over_high = left_over.astype(BF16)
    over_low = (left_over - over_high.astype(F32)).astype(BF16)
    over = jnp.concatenate([over_high, over_low, jnp.zeros((14, width), BF16)], axis=0)
    shift = scale * (line(1) - mean)
    noise = jnp.concatenate([mine_ref[...], got_ref[:, here]], axis=0)
    right = shift + factor * noise
    high = right.astype(BF16)
    low = (right - high.astype(F32)).astype(BF16)
    left = jnp.concatenate([spreads[0], high, low, over], axis=0)
    at_over = dot_nt(left, over)
    at_over = at_over[:, 0:1] + at_over[:, 1:2]
    gram_over = at_over[0:rows]
    cross_over = at_over[rows : 2 * rows] + at_over[2 * rows : 3 * rows]
    both = at_over[3 * rows : 3 * rows + 1] + at_over[3 * rows + 1 : 3 * rows + 2]
    for i in range(4):
        part = dot_nt(left, spreads[i])
        over_row = part[3 * rows : 3 * rows + 1] + part[3 * rows + 1 : 3 * rows + 2]
        gram = part[0:rows] - gram_over - (over_row - both)
        cross = part[rows : 2 * rows] + part[2 * rows : 3 * rows] - cross_over
        own_ref[i, 0:half, :] = gram[0:half]
        own_ref[i, half:rows, :] = cross[0:half]
        other_ref[i, 0:half, :] = pltpu.roll(gram[half:rows], half, 1)
        other_ref[i, half:rows, :] = pltpu.roll(cross[half:rows], half, 1)


def local_ids(ids_ref, place, k):
    chip = lax.rem(lax.div(place, 2) + 4 - k, 4)
    ids = ids_ref[pl.ds(chip, 1), :]
    return jnp.where(lax.rem(place, 2) == 1, pltpu.roll(ids, 64, 1), ids)


def local_members(place, k, rows):
    chip = lax.rem(lax.div(place, 2) + 4 - k, 4)
    lane = lax.broadcasted_iota(jnp.int32, (rows, 128), 1)
    return chip * 128 + lax.rem(lane + 64 * lax.rem(place, 2), 128)


def begin_kernel(place_ref, ids_ref, own_ref, other_ref, inverse_ref, upper_ref, row_ref, m_ref):
    half, block = 64, 128
    place = place_ref[0]
    def piece(i):
        return jnp.concatenate([own_ref[i, 0:half, :], pltpu.roll(other_ref[i], half, 1)], axis=0)

    inverse = invert_block(piece(0) + unit_block(block, block))
    inverse_ref[...] = inverse
    for i in range(1, 4):
        row_ref[:, (i - 1) * block : i * block] = piece(i)
    upper = dot_nn(inverse, row_ref[...], EXACT)
    upper_ref[...] = upper
    members = place * half + lax.broadcasted_iota(jnp.int32, (half, block), 0)
    for i in range(4):
        match = (local_ids(ids_ref, place, i) == members.astype(F32)).astype(F32)
        m_ref[:, i * block : (i + 1) * block] = own_ref[i, half:block, :] + match
    m_ref[:, block:] = m_ref[:, block:] - dot_nn(m_ref[:, :block], upper, EXACT)


def solve_kernel(
    place_ref, ids_ref, inverse_ref, upper_ref, row_ref, right_ref,
    g1_ref, g2_ref, g3_ref, theirs_ref, *rest
):
    fields, (out_ref, anomaly_ref, m_ref) = rest[:-3], rest[-3:]
    size, block, half = 512, 128, 64
    place = place_ref[0]
    unit = unit_block(block, block)

    def piece(mine, k, i):
        return jnp.concatenate([mine[i], pltpu.roll(theirs_ref[2 * (k - 1) + i], half, 1)], axis=0)

    def centre(strip):
        here = slice(strip * block, (strip + 1) * block)
        sums = [jnp.sum(ref[:, here].astype(F32), axis=0, keepdims=True) for ref in fields]
        mean = tree_sum(sums) / size
        at = 0
        for ref in fields:
            anomaly_ref[at : at + ref.shape[0], here] = (ref[:, here].astype(F32) - mean).astype(BF16)
            at += ref.shape[0]

    strips = anomaly_ref.shape[1] // block

    def beside(b, t):
        step = (b - 1) * 16 + t
        for strip in range(step * strips // 48, (step + 1) * strips // 48):
            centre(strip)

    upper = upper_ref[...]
    row = row_ref[...]
    m_ref[...] = right_ref[...]
    a = {
        (1, 1): piece(g1_ref, 1, 0) + unit,
        (1, 2): piece(g1_ref, 1, 1),
        (2, 2): piece(g2_ref, 2, 0) + unit,
        (2, 3): piece(g2_ref, 2, 1),
        (3, 3): piece(g3_ref, 3, 0) + unit,
        (1, 3): piece(g3_ref, 3, 1).T,
    }
    inverses, uppers = {0: inverse_ref[...]}, {0: upper}
    for b in range(4):
        hi = (b + 1) * block
        if b:
            inverses[b] = invert_block(a[b, b], functools.partial(beside, b))
            if hi < size:
                row = jnp.concatenate([a[b, j] for j in range(b + 1, 4)], axis=1)
                upper = dot_nn(inverses[b], row, EXACT)
                uppers[b] = upper
                m_ref[:, hi:] = m_ref[:, hi:] - dot_nn(m_ref[:, hi - block : hi], upper, EXACT)
        for i in range(b + 1, 4):
            left = row[:, (i - b - 1) * block : (i - b) * block]
            change = dot_tn(left, upper[:, (i - b - 1) * block :], EXACT)
            for j in range(i, 4):
                a[i, j] = a[i, j] - change[:, (j - i) * block : (j - i + 1) * block]
    for b in range(3, -1, -1):
        lo, hi = b * block, (b + 1) * block
        z = dot_nn(m_ref[:, lo:hi], inverses[b], EXACT)
        if hi < size:
            z = z - dot_nt(m_ref[:, hi:size], uppers[b], EXACT)
        m_ref[:, lo:hi] = z

    columns = jnp.concatenate(
        [jnp.broadcast_to(local_ids(ids_ref, place, k), (block, block)).T for k in range(4)], axis=0
    )
    own = place * half + lax.broadcasted_iota(jnp.int32, (half, block), 0)
    for k in range(4):
        match = (columns == local_members(place, k, size).astype(F32)).astype(F32)
        ordered = dot_nn(m_ref[...], match, EXACT)
        own_unit = (own == local_members(place, k, half)).astype(F32)
        out_ref[:, k * block : (k + 1) * block] = (ordered - own_unit).astype(BF16)


def update_kernel(t_ref, field_ref, anomaly_ref, out_ref):
    wide = 1024
    for at in range(0, out_ref.shape[1], wide):
        here = slice(at, at + wide)
        increment = dot_nn(t_ref[...], anomaly_ref[:, here])
        out_ref[:, here] = (field_ref[:, here].astype(F32) + increment).astype(BF16)


def body(members_field, predicted, noise, observed, obs_precision, obs_block, block_error_scale, member_ids):
    rows, width = predicted.shape
    members = member_ids.shape[0]
    cells = members_field.shape[1]
    half = width // 2
    factor = float(1.0 / (members - 1) ** 0.5)
    place = lax.axis_index("ens").reshape(1).astype(jnp.int32)
    swap = [(i, i ^ 1) for i in range(8)]
    smem = pl.BlockSpec(memory_space=pltpu.SMEM)
    vmem = pl.BlockSpec(memory_space=pltpu.VMEM)

    def room(mib):
        return pltpu.CompilerParams(vmem_limit_bytes=mib * MIB)

    def shaped(*shape, dtype=F32):
        return jax.ShapeDtypeStruct(shape, dtype)

    def turned(array, steps):
        return lax.ppermute(array, "ens", [(i, (i + 2 * steps) % 8) for i in range(8)])

    def swapped(array):
        return lax.ppermute(array, "ens", swap)

    pred_got = swapped(predicted)
    core = lax.rem(lax.axis_index("ens"), 2)
    pred_mine = lax.dynamic_slice_in_dim(predicted, core * half, half, 1)
    payload = pl.pallas_call(
        prepare_kernel,
        out_shape=shaped(2 * rows + 16, half, dtype=BF16),
        in_specs=[smem, vmem, vmem],
        compiler_params=room(32),
        name="prepare",
    )(place, pred_mine, pred_got)
    payload, noise, member_ids, obs_precision, observed, obs_block, block_error_scale = lax.optimization_barrier(
        (payload, noise, member_ids, obs_precision, observed, obs_block, block_error_scale)
    )
    noise_got = swapped(noise)
    noise_mine = lax.dynamic_slice_in_dim(noise, core * half, half, 1)
    facts = jnp.stack([a.reshape(-1, 128).astype(F32) for a in (obs_precision, observed, obs_block)])
    table = jnp.pad(block_error_scale, (0, 128 - block_error_scale.shape[0])).reshape(1, 128)
    payloads = [payload] + [turned(payload, k) for k in (1, 2, 3)]

    members_field, *payloads[3:] = lax.optimization_barrier((members_field, payloads[3]))
    ahead = turned(members_field, 3)

    ids = member_ids.astype(F32).reshape(4, 128)
    after_spread = lax.optimization_barrier((members_field, noise_mine, ids, facts, table, *payloads))
    (field, noise_mine, ids, facts, table), payloads = after_spread[:5], after_spread[5:]
    back = turned(field, 1)

    own, other = pl.pallas_call(
        functools.partial(gram_kernel, factor=factor),
        out_shape=(shaped(4, 2 * rows, 2 * rows),) * 2,
        in_specs=[smem] + [vmem] * 8,
        compiler_params=room(8),
        name="gram",
    )(place, *payloads, noise_mine, noise_got, facts, table)
    part = own + swapped(other)

    spread_out = lax.all_to_all(part.reshape(32, 16, 128), "space", split_axis=0, concat_axis=0)
    summed = jnp.sum(spread_out, axis=0)
    summed, back, ahead, near_field = lax.optimization_barrier((summed, back, ahead, field))
    cut = rows // 2
    beyond = [turned(back[:cut], 1), turned(ahead[cut:], 3)]
    others = [swapped(back), swapped(ahead), swapped(near_field)]
    whole = lax.all_to_all(
        jnp.broadcast_to(summed[None], (32, 16, 128)), "space", split_axis=0, concat_axis=0
    ).reshape(4, 2 * rows, 2 * rows)

    whole, *moved = lax.optimization_barrier((whole, *beyond, *others))
    beyond, others = moved[:2], moved[2:]
    gram = whole[:, :rows]
    near = gram[0:2]
    far = jnp.stack([gram[0], gram[2]])
    grams = [turned(near, 1), turned(near, 2), turned(far, 3)]
    gram_other = swapped(gram)
    beyond_others = [swapped(f) for f in beyond]
    inverse, upper, row, right = pl.pallas_call(
        begin_kernel,
        out_shape=(
            shaped(128, 128),
            shaped(128, 384),
            shaped(128, 384),
            shaped(rows, members),
        ),
        in_specs=[smem, vmem, vmem, vmem],
        compiler_params=room(8),
        name="begin",
    )(place, ids, whole, gram_other)
    inverse, *grams = lax.optimization_barrier((inverse, *grams))
    theirs = swapped(jnp.concatenate(grams, axis=0))
    fields = [field, others[2], back, others[0], *beyond, *beyond_others, ahead, others[1]]
    transform, anomaly = pl.pallas_call(
        solve_kernel,
        out_shape=(shaped(rows, members, dtype=BF16), shaped(members, cells, dtype=BF16)),
        in_specs=[smem] + [vmem] * (9 + len(fields)),
        scratch_shapes=[pltpu.VMEM((rows, members), F32)],
        compiler_params=room(22),
        name="solve",
    )(place, ids, inverse, upper, row, right, *grams, theirs, *fields)
    return pl.pallas_call(
        update_kernel,
        out_shape=shaped(rows, cells, dtype=BF16),
        in_specs=[vmem] * 3,
        compiler_params=room(14),
        name="update",
    )(transform, field, anomaly)


def solution(mesh):
    placed = (
        P("ens", "space"),
        P("ens", "space"),
        P("ens", "space"),
        P("space"),
        P("space"),
        P("space"),
        P(),
        P(),
    )
    return jax.shard_map(
        body, mesh=mesh, in_specs=placed, out_specs=P("ens", "space"), check_vma=False
    )
```

```python
import functools
import jax
import jax.numpy as jnp
from jax import lax
from jax.experimental import pallas as pl
from jax.experimental.pallas import tpu as pltpu
from jax.sharding import PartitionSpec as P

F32 = jnp.float32
BF16 = jnp.bfloat16
EXACT = lax.Precision.HIGHEST
MIB = 1024 * 1024


def across_rows(tile, row):
    return jnp.broadcast_to(tile[row : row + 1, :], tile.shape)


def across_lanes(tile, lane):
    return jnp.broadcast_to(tile[:, lane : lane + 1], tile.shape)


def dot_nt(a, b, precision=None):
    return lax.dot_general(
        a, b, (((1,), (1,)), ((), ())), precision=precision, preferred_element_type=F32
    )


def dot_tn(a, b, precision=None):
    return lax.dot_general(
        a, b, (((0,), (0,)), ((), ())), precision=precision, preferred_element_type=F32
    )


def dot_nn(a, b, precision=None):
    return jnp.dot(a, b, precision=precision, preferred_element_type=F32)


def tree_sum(terms):
    while len(terms) > 1:
        terms = [terms[i] + terms[i + 1] if i + 1 < len(terms) else terms[i] for i in range(0, len(terms), 2)]
    return terms[0]


def unit_block(rows, cols):
    at = lax.broadcasted_iota(jnp.int32, (rows, cols), 0)
    return (at == lax.broadcasted_iota(jnp.int32, (rows, cols), 1)).astype(F32)


def invert_block(block, beside=None):
    lanes = lax.broadcasted_iota(jnp.int32, (8, 128), 1)
    subs = lax.broadcasted_iota(jnp.int32, (8, 128), 0)
    tiles = [block[8 * i : 8 * i + 8, :] for i in range(16)]
    for t in range(16):
        old = tiles[t]
        cols = [across_lanes(old, 8 * t + j) for j in range(8)]
        panel = (lanes >= 8 * t) & (lanes < 8 * t + 8)
        old = jnp.where(panel, (lanes - 8 * t == subs).astype(F32), old)
        olds = [across_rows(old, j) for j in range(8)]
        for k in range(8):
            recip = 1.0 / across_rows(cols[k], k)
            pivot = cols[k]
            here = subs == k
            for j in range(8):
                if j != k:
                    scaled = across_rows(cols[j], k) * recip
                    cols[j] = jnp.where(here, scaled, cols[j] - pivot * scaled)
            cols[k] = jnp.where(here, recip, -pivot * recip)
        row = tree_sum([cols[j] * olds[j] for j in range(8)])
        rows = [across_rows(row, j) for j in range(8)]
        for i in [(t + 1 + n) % 16 for n in range(15)]:
            total = tree_sum([across_lanes(tiles[i], 8 * t + j) * rows[j] for j in range(8)])
            tiles[i] = jnp.where(panel, 0.0, tiles[i]) - total
        tiles[t] = row
        if beside is not None:
            beside(t)
    return jnp.concatenate(tiles, axis=0)


def prepare_kernel(place_ref, mine_ref, got_ref, out_ref):
    half = mine_ref.shape[0]
    rows = 2 * half
    width = out_ref.shape[1]
    here = pl.ds(pl.multiple_of(lax.rem(place_ref[0], 2) * width, 128), width)
    mine = mine_ref[...]
    got = got_ref[:, here]
    mean = (jnp.sum(mine, axis=0, keepdims=True) + jnp.sum(got, axis=0, keepdims=True)) / rows
    out_ref[0:half, :] = (mine - mean).astype(BF16)
    out_ref[half:rows, :] = (got - mean).astype(BF16)
    high = mean.astype(BF16)
    rest = mean - high.astype(F32)
    mid = rest.astype(BF16)
    low = (rest - mid.astype(F32)).astype(BF16)
    out_ref[rows : rows + 16, :] = jnp.concatenate([high, mid, low, jnp.zeros((13, width), BF16)], axis=0)


def gram_kernel(
    place_ref, p0_ref, p1_ref, p2_ref, p3_ref, mine_ref, got_ref, facts_ref, table_ref, own_ref, other_ref, *, factor
):
    refs = (p0_ref, p1_ref, p2_ref, p3_ref)
    rows = p0_ref.shape[0] - 16
    half = rows // 2
    width = p0_ref.shape[1]
    core = lax.rem(place_ref[0], 2)
    here = pl.ds(pl.multiple_of(core * width, 128), width)

    def line(which):
        count = width // 128
        return jnp.concatenate([facts_ref[which, pl.ds(core * count + j, 1), :] for j in range(count)], axis=1)

    block = line(2)
    error_scale = jnp.zeros_like(block)
    for b in range(32):
        level = jnp.broadcast_to(table_ref[:, b : b + 1], block.shape)
        error_scale = jnp.where(block == float(b), level, error_scale)
    scale = line(0) / error_scale * factor
    means = []
    for ref in refs:
        tail = ref[rows : rows + 16, :].astype(F32)
        means.append(tail[0:1, :] + (tail[1:2, :] + tail[2:3, :]))
    mean = ((means[0] + means[1]) + (means[2] + means[3])) * 0.25
    spreads = [
        (scale * (ref[0:rows, :].astype(F32) + (m - mean))).astype(BF16) for ref, m in zip(refs, means)
    ]
    left_over = tree_sum([jnp.sum(s.astype(F32), axis=0, keepdims=True) for s in spreads]) / (4 * rows)
    over_high = left_over.astype(BF16)
    over_low = (left_over - over_high.astype(F32)).astype(BF16)
    over = jnp.concatenate([over_high, over_low, jnp.zeros((14, width), BF16)], axis=0)
    shift = scale * (line(1) - mean)
    noise = jnp.concatenate([mine_ref[...], got_ref[:, here]], axis=0)
    right = shift + factor * noise
    high = right.astype(BF16)
    low = (right - high.astype(F32)).astype(BF16)
    left = jnp.concatenate([spreads[0], high, low, over], axis=0)
    at_over = dot_nt(left, over)
    at_over = at_over[:, 0:1] + at_over[:, 1:2]
    gram_over = at_over[0:rows]
    cross_over = at_over[rows : 2 * rows] + at_over[2 * rows : 3 * rows]
    both = at_over[3 * rows : 3 * rows + 1] + at_over[3 * rows + 1 : 3 * rows + 2]
    for i in range(4):
        part = dot_nt(left, spreads[i])
        over_row = part[3 * rows : 3 * rows + 1] + part[3 * rows + 1 : 3 * rows + 2]
        gram = part[0:rows] - gram_over - (over_row - both)
        cross = part[rows : 2 * rows] + part[2 * rows : 3 * rows] - cross_over
        own_ref[i, 0:half, :] = gram[0:half]
        own_ref[i, half:rows, :] = cross[0:half]
        other_ref[i, 0:half, :] = pltpu.roll(gram[half:rows], half, 1)
        other_ref[i, half:rows, :] = pltpu.roll(cross[half:rows], half, 1)


def local_ids(ids_ref, place, k):
    chip = lax.rem(lax.div(place, 2) + 4 - k, 4)
    ids = ids_ref[pl.ds(chip, 1), :]
    return jnp.where(lax.rem(place, 2) == 1, pltpu.roll(ids, 64, 1), ids)


def local_members(place, k, rows):
    chip = lax.rem(lax.div(place, 2) + 4 - k, 4)
    lane = lax.broadcasted_iota(jnp.int32, (rows, 128), 1)
    return chip * 128 + lax.rem(lane + 64 * lax.rem(place, 2), 128)


def begin_kernel(place_ref, ids_ref, own_ref, other_ref, inverse_ref, upper_ref, row_ref, m_ref):
    half, block = 64, 128
    place = place_ref[0]
    def piece(i):
        return jnp.concatenate([own_ref[i, 0:half, :], pltpu.roll(other_ref[i], half, 1)], axis=0)

    inverse = invert_block(piece(0) + unit_block(block, block))
    inverse_ref[...] = inverse
    for i in range(1, 4):
        row_ref[:, (i - 1) * block : i * block] = piece(i)
    upper = dot_nn(inverse, row_ref[...], EXACT)
    upper_ref[...] = upper
    members = place * half + lax.broadcasted_iota(jnp.int32, (half, block), 0)
    for i in range(4):
        match = (local_ids(ids_ref, place, i) == members.astype(F32)).astype(F32)
        m_ref[:, i * block : (i + 1) * block] = own_ref[i, half:block, :] + match
    m_ref[:, block:] = m_ref[:, block:] - dot_nn(m_ref[:, :block], upper, EXACT)


def solve_kernel(
    place_ref, ids_ref, inverse_ref, upper_ref, row_ref, right_ref,
    g1_ref, g2_ref, g3_ref, theirs_ref, *rest
):
    fields, (out_ref, anomaly_ref, m_ref) = rest[:-3], rest[-3:]
    size, block, half = 512, 128, 64
    place = place_ref[0]
    unit = unit_block(block, block)

    def piece(mine, k, i):
        return jnp.concatenate([mine[i], pltpu.roll(theirs_ref[2 * (k - 1) + i], half, 1)], axis=0)

    def centre(strip):
        here = slice(strip * block, (strip + 1) * block)
        sums = [jnp.sum(ref[:, here].astype(F32), axis=0, keepdims=True) for ref in fields]
        mean = tree_sum(sums) / size
        at = 0
        for ref in fields:
            anomaly_ref[at : at + ref.shape[0], here] = (ref[:, here].astype(F32) - mean).astype(BF16)
            at += ref.shape[0]

    strips = anomaly_ref.shape[1] // block

    def beside(b, t):
        step = (b - 1) * 16 + t
        for strip in range(step * strips // 48, (step + 1) * strips // 48):
            centre(strip)

    upper = upper_ref[...]
    row = row_ref[...]
    m_ref[...] = right_ref[...]
    a = {
        (1, 1): piece(g1_ref, 1, 0) + unit,
        (1, 2): piece(g1_ref, 1, 1),
        (2, 2): piece(g2_ref, 2, 0) + unit,
        (2, 3): piece(g2_ref, 2, 1),
        (3, 3): piece(g3_ref, 3, 0) + unit,
        (1, 3): piece(g3_ref, 3, 1).T,
    }
    inverses, uppers = {0: inverse_ref[...]}, {0: upper}
    for b in range(4):
        hi = (b + 1) * block
        if b:
            inverses[b] = invert_block(a[b, b], functools.partial(beside, b))
            if hi < size:
                row = jnp.concatenate([a[b, j] for j in range(b + 1, 4)], axis=1)
                upper = dot_nn(inverses[b], row, EXACT)
                uppers[b] = upper
                m_ref[:, hi:] = m_ref[:, hi:] - dot_nn(m_ref[:, hi - block : hi], upper, EXACT)
        for i in range(b + 1, 4):
            left = row[:, (i - b - 1) * block : (i - b) * block]
            change = dot_tn(left, upper[:, (i - b - 1) * block :], EXACT)
            for j in range(i, 4):
                a[i, j] = a[i, j] - change[:, (j - i) * block : (j - i + 1) * block]
    for b in range(3, -1, -1):
        lo, hi = b * block, (b + 1) * block
        z = dot_nn(m_ref[:, lo:hi], inverses[b], EXACT)
        if hi < size:
            z = z - dot_nt(m_ref[:, hi:size], uppers[b], EXACT)
        m_ref[:, lo:hi] = z

    columns = jnp.concatenate(
        [jnp.broadcast_to(local_ids(ids_ref, place, k), (block, block)).T for k in range(4)], axis=0
    )
    own = place * half + lax.broadcasted_iota(jnp.int32, (half, block), 0)
    for k in range(4):
        match = (columns == local_members(place, k, size).astype(F32)).astype(F32)
        ordered = dot_nn(m_ref[...], match, EXACT)
        own_unit = (own == local_members(place, k, half)).astype(F32)
        out_ref[:, k * block : (k + 1) * block] = (ordered - own_unit).astype(BF16)


def update_kernel(t_ref, field_ref, anomaly_ref, out_ref):
    wide = 1024
    for at in range(0, out_ref.shape[1], wide):
        here = slice(at, at + wide)
        increment = dot_nn(t_ref[...], anomaly_ref[:, here])
        out_ref[:, here] = (field_ref[:, here].astype(F32) + increment).astype(BF16)


def body(members_field, predicted, noise, observed, obs_precision, obs_block, block_error_scale, member_ids):
    rows, width = predicted.shape
    members = member_ids.shape[0]
    cells = members_field.shape[1]
    half = width // 2
    factor = float(1.0 / (members - 1) ** 0.5)
    place = lax.axis_index("ens").reshape(1).astype(jnp.int32)
    swap = [(i, i ^ 1) for i in range(8)]
    smem = pl.BlockSpec(memory_space=pltpu.SMEM)
    vmem = pl.BlockSpec(memory_space=pltpu.VMEM)

    def room(mib):
        return pltpu.CompilerParams(vmem_limit_bytes=mib * MIB)

    def shaped(*shape, dtype=F32):
        return jax.ShapeDtypeStruct(shape, dtype)

    def turned(array, steps):
        return lax.ppermute(array, "ens", [(i, (i + 2 * steps) % 8) for i in range(8)])

    def swapped(array):
        return lax.ppermute(array, "ens", swap)

    pred_got = swapped(predicted)
    core = lax.rem(lax.axis_index("ens"), 2)
    pred_mine = lax.dynamic_slice_in_dim(predicted, core * half, half, 1)
    payload = pl.pallas_call(
        prepare_kernel,
        out_shape=shaped(2 * rows + 16, half, dtype=BF16),
        in_specs=[smem, vmem, vmem],
        compiler_params=room(32),
        name="prepare",
    )(place, pred_mine, pred_got)
    payload, noise, member_ids, obs_precision, observed, obs_block, block_error_scale = lax.optimization_barrier(
        (payload, noise, member_ids, obs_precision, observed, obs_block, block_error_scale)
    )
    noise_got = swapped(noise)
    noise_mine = lax.dynamic_slice_in_dim(noise, core * half, half, 1)
    facts = jnp.stack([a.reshape(-1, 128).astype(F32) for a in (obs_precision, observed, obs_block)])
    table = jnp.pad(block_error_scale, (0, 128 - block_error_scale.shape[0])).reshape(1, 128)
    payloads = [payload] + [turned(payload, k) for k in (1, 2, 3)]

    members_field, *payloads[3:] = lax.optimization_barrier((members_field, payloads[3]))
    ahead = turned(members_field, 3)

    ids = member_ids.astype(F32).reshape(4, 128)
    after_spread = lax.optimization_barrier((members_field, noise_mine, ids, facts, table, *payloads))
    (field, noise_mine, ids, facts, table), payloads = after_spread[:5], after_spread[5:]
    back = turned(field, 1)

    own, other = pl.pallas_call(
        functools.partial(gram_kernel, factor=factor),
        out_shape=(shaped(4, 2 * rows, 2 * rows),) * 2,
        in_specs=[smem] + [vmem] * 8,
        compiler_params=room(8),
        name="gram",
    )(place, *payloads, noise_mine, noise_got, facts, table)
    part = own + swapped(other)

    spread_out = lax.all_to_all(part.reshape(32, 16, 128), "space", split_axis=0, concat_axis=0)
    summed = jnp.sum(spread_out, axis=0)
    summed, back, ahead, near_field = lax.optimization_barrier((summed, back, ahead, field))
    cut = rows // 2
    low, high, back, ahead, near_field = lax.optimization_barrier((back[:cut], ahead[cut:], back, ahead, near_field))
    beyond = [turned(low, 1), turned(high, 3)]
    others = [swapped(back), swapped(ahead), swapped(near_field)]
    whole = lax.all_to_all(
        jnp.broadcast_to(summed[None], (32, 16, 128)), "space", split_axis=0, concat_axis=0
    ).reshape(4, 2 * rows, 2 * rows)

    whole, *moved = lax.optimization_barrier((whole, *beyond, *others))
    beyond, others = moved[:2], moved[2:]
    gram = whole[:, :rows]
    near = gram[0:2]
    far = jnp.stack([gram[0], gram[2]])
    grams = [turned(near, 1), turned(near, 2), turned(far, 3)]
    gram_other = swapped(gram)
    beyond_others = [swapped(f) for f in beyond]
    inverse, upper, row, right = pl.pallas_call(
        begin_kernel,
        out_shape=(
            shaped(128, 128),
            shaped(128, 384),
            shaped(128, 384),
            shaped(rows, members),
        ),
        in_specs=[smem, vmem, vmem, vmem],
        compiler_params=room(8),
        name="begin",
    )(place, ids, whole, gram_other)
    inverse, *grams = lax.optimization_barrier((inverse, *grams))
    theirs = swapped(jnp.concatenate(grams, axis=0))
    fields = [field, others[2], back, others[0], *beyond, *beyond_others, ahead, others[1]]
    transform, anomaly = pl.pallas_call(
        solve_kernel,
        out_shape=(shaped(rows, members, dtype=BF16), shaped(members, cells, dtype=BF16)),
        in_specs=[smem] + [vmem] * (9 + len(fields)),
        scratch_shapes=[pltpu.VMEM((rows, members), F32)],
        compiler_params=room(22),
        name="solve",
    )(place, ids, inverse, upper, row, right, *grams, theirs, *fields)
    return pl.pallas_call(
        update_kernel,
        out_shape=shaped(rows, cells, dtype=BF16),
        in_specs=[vmem] * 3,
        compiler_params=room(14),
        name="update",
    )(transform, field, anomaly)


def solution(mesh):
    placed = (
        P("ens", "space"),
        P("ens", "space"),
        P("ens", "space"),
        P("space"),
        P("space"),
        P("space"),
        P(),
        P(),
    )
    return jax.shard_map(
        body, mesh=mesh, in_specs=placed, out_specs=P("ens", "space"), check_vma=False
    )
```
